32 devices in a mesh: grp: 2 (over x), dap: 16 (over z, y, core).
Axes of the slice: x: 2, y: 2, z: 4, core: 2. Of those that a mesh axis runs over, the one named last changes fastest.
Arguments:
- alignment_rows: bfloat16 [32, 768, 256], P(('grp', 'dap')), parts along dimension 0, may hold values from -6 to 6
- norm_gain_vector: float32 [256], replicated, may hold values from 0.5 to 1.5
- norm_bias_vector: float32 [256], replicated, may hold values from -2 to 2
- left_weight: bfloat16 [256, 32], replicated, may hold values from -0.375 to 0.375
- right_weight: bfloat16 [256, 32], replicated, may hold values from -0.375 to 0.375
- output_weight: bfloat16 [1024, 128], replicated, may hold values from -0.1875 to 0.1875
- pair_output_gradient: bfloat16 [1536, 768, 128], P(('grp', 'dap')), parts along dimension 0, may hold values from -6 to 6
- sequence_real_mask: int32 [32], P('grp'), parts along dimension 0, may hold values 0 or 1
- sequence_chain_index: int32 [32], P('grp'), parts along dimension 0, may hold values from 0 to 4
- residue_real_mask: int32 [1536], P('grp'), parts along dimension 0, may hold values 0 or 1
- residue_chain_index: int32 [1536], P('grp'), parts along dimension 0, may hold values from 0 to 3, never falling along the last dimension, each value on 1 to 384 neighbouring positions
Outputs:
- alignment_gradient: bfloat16 [32, 768, 256], P(('grp', 'dap')), parts along dimension 0
- norm_gain_gradient: float32 [512], P('grp'), parts along dimension 0
- norm_bias_gradient: float32 [512], P('grp'), parts along dimension 0
- left_weight_gradient: float32 [512, 32], P('grp'), parts along dimension 0
- right_weight_gradient: float32 [512, 32], P('grp'), parts along dimension 0
- output_weight_gradient: float32 [2048, 128], P('grp'), parts along dimension 0
The draws below stay inside these ranges and needn't reach their ends.
There are 2 independent parts, one for each index of `grp`. The reference program is written for one: setup_inputs(seed, part) draws one part's arguments, and reference() takes and returns one part's arrays. A program takes and returns all parts, laid end to end along the dimension named above; an argument that names none is the same for every part. Nothing has to cross between parts.
All inputs are finite; a program needn't handle non-finite values.
Results may differ from the reference program's by a relative error of at most 0.0075.
Values may be sent and summed in bfloat16 or wider, within the bound.
No kernel may reach another device: no remote copies, remote signals or barrier semaphores. Data moves between devices by JAX's collectives and lax.ppermute only.
A program may use at most 256 MiB of HBM per device.

```python
import math
import jax
import jax.numpy as jnp
import numpy as np
from jax import lax

ALIGNMENT_WIDTH = 256
PROJECTION_SIZE = 32
PAIR = 128
RESIDUE_COUNT = 768
CHAINS = 4
SEQUENCE_COUNT = 16


def with_ends(drawn, rng, low, high):
    longest = drawn.shape.index(max(drawn.shape))
    spots = []
    for shift in (0, 1):
        where = [jax.random.randint(jax.random.fold_in(rng, axis), (), 0, length) for axis, length in enumerate(drawn.shape)]
        where[longest] = (where[longest] + shift) % drawn.shape[longest]
        spots.append(tuple(where))
    return drawn.at[spots[0]].set(low).at[spots[1]].set(high)


def block_levels(own_key, shape, shards, least, high):
    loudness = 1.0
    for position, parts in shards:
        steps = jax.random.uniform(jax.random.fold_in(jax.random.fold_in(own_key, 6), position), (parts,), jnp.float32, least / len(shards), high / len(shards))
        loudness = loudness * jnp.repeat(jnp.exp(steps), shape[position] // parts).reshape((-1,) + (1,) * (len(shape) - 1 - position))
    return loudness


def profile(count, total, limit, lean):
    loads = [(1 << 20) // math.isqrt(rank ** lean) + 1 for rank in range(2, count + 1)]
    surplus, counts = total - limit - (count - 1), [1] * (count - 1)
    while surplus > 0:
        candidates = [i for i in range(count - 1) if counts[i] < limit]
        mass, left = sum([loads[i] for i in candidates]), surplus
        for i in candidates:
            addition = min(limit - counts[i], max(1, left * loads[i] // mass), surplus)
            counts[i] = counts[i] + addition
            surplus = surplus - addition
    return np.array([limit] + counts)


def ragged_sizes(stream_key, count, total, bound, lean):
    if count == 2:
        one = jax.random.randint(stream_key, (), max(1, total - bound), min(bound, total - 1) + 1)
        return jnp.stack([one, total - one])
    tallies = jnp.asarray(profile(count, total, bound, lean), jnp.int32)
    twos = (count - 1) // 2
    donor, sink = tallies[1:1 + 2 * twos:2], tallies[2:2 + 2 * twos:2]
    room = jnp.minimum(donor - 1, bound - sink)
    moved = jax.random.randint(jax.random.fold_in(stream_key, 1), (twos,), 0, 1 << 20) % (room + 1)
    tallies = tallies.at[1:1 + 2 * twos:2].set(donor - moved).at[2:2 + 2 * twos:2].set(sink + moved)
    return tallies[jax.random.permutation(jax.random.fold_in(stream_key, 2), count)]


def normal_values(rng, shape, scale, most, shards=(), held_as=jnp.bfloat16):
    factor_of = block_levels(rng, shape, shards, -0.22, 0.18) if shards else 1.0
    values = jax.random.normal(rng, shape, jnp.float32) * scale * factor_of
    return jnp.minimum(jnp.maximum(values, -most), most).astype(held_as)


def setup_inputs(seed: int = 0, part: int = 0) -> dict:
    seeds = jax.random.split(jax.random.key(seed), 12)
    part_keys = jax.random.split(jax.random.fold_in(seeds[11], part), 12)
    return {
        "alignment_rows": normal_values(part_keys[0], (SEQUENCE_COUNT, RESIDUE_COUNT, ALIGNMENT_WIDTH), 1.0, 6.0, ((0, 16),)),
        "norm_gain_vector": jnp.clip(1.0 + 0.1 * jax.random.normal(seeds[1], (ALIGNMENT_WIDTH,), jnp.float32), 0.5, 1.5),
        "norm_bias_vector": normal_values(seeds[2], (ALIGNMENT_WIDTH,), 0.3, 2.0, (), jnp.float32),
        "left_weight": normal_values(seeds[3], (ALIGNMENT_WIDTH, PROJECTION_SIZE), ALIGNMENT_WIDTH ** -0.5, 0.375),
        "right_weight": normal_values(seeds[4], (ALIGNMENT_WIDTH, PROJECTION_SIZE), ALIGNMENT_WIDTH ** -0.5, 0.375),
        "output_weight": normal_values(seeds[5], (PROJECTION_SIZE * PROJECTION_SIZE, PAIR), (PROJECTION_SIZE * PROJECTION_SIZE) ** -0.5, 0.1875),
        "pair_output_gradient": normal_values(part_keys[6], (RESIDUE_COUNT, RESIDUE_COUNT, PAIR), 1.0, 6.0, ((0, 16),)),
        "sequence_real_mask": with_ends((jax.random.randint(part_keys[7], (SEQUENCE_COUNT,), 0, 8) < 7).astype(jnp.int32), jax.random.fold_in(part_keys[7], 1), 0, 1),
        "sequence_chain_index": with_ends(jax.random.randint(part_keys[8], (SEQUENCE_COUNT,), 0, CHAINS + 1), jax.random.fold_in(part_keys[8], 1), 0, CHAINS).astype(jnp.int32),
        "residue_real_mask": with_ends((jax.random.randint(part_keys[9], (RESIDUE_COUNT,), 0, 16) < 15).astype(jnp.int32), jax.random.fold_in(part_keys[9], 1), 0, 1),
        "residue_chain_index": jnp.searchsorted(jnp.cumsum(ragged_sizes(part_keys[10], CHAINS, RESIDUE_COUNT, RESIDUE_COUNT // 2, 0)), jnp.arange(RESIDUE_COUNT), side="right").astype(jnp.int32),
    }


EPSILON = 1e-05
BLOCK_RES = 32

def coverage_of(sequence_real_mask, sequence_chain_index, residue_real_mask, residue_chain_index):
    paired = sequence_chain_index[:, None] == CHAINS
    same_chain = sequence_chain_index[:, None] == residue_chain_index[None, :]
    covered = jnp.where(paired | same_chain, 1.0, 0.0).astype(jnp.float32)
    return covered * sequence_real_mask[:, None].astype(jnp.float32) * residue_real_mask[None, :].astype(jnp.float32)

def rounded(values):
    return lax.optimization_barrier(values.astype(jnp.bfloat16)).astype(jnp.float32)

def reference(alignment_rows, norm_gain_vector, norm_bias_vector, left_weight, right_weight, output_weight, pair_output_gradient, sequence_real_mask, sequence_chain_index, residue_real_mask, residue_chain_index):
    coverage = coverage_of(sequence_real_mask, sequence_chain_index, residue_real_mask, residue_chain_index)
    input_tensors = alignment_rows.astype(jnp.float32)
    center = input_tensors - lax.optimization_barrier(jnp.mean(input_tensors, axis=-1, keepdims=True))
    spread = lax.optimization_barrier(jnp.mean(center * center, axis=-1, keepdims=True))
    inverse_deviation = lax.rsqrt(spread + EPSILON)
    single_entry = center * inverse_deviation
    normed = (single_entry * norm_gain_vector + norm_bias_vector).astype(jnp.bfloat16)
    normed_f = normed.astype(jnp.float32)
    left = (jnp.einsum('sif,fc->sci', normed_f, left_weight.astype(jnp.float32)) * coverage[:, None, :]).astype(jnp.bfloat16)
    right = (jnp.einsum('sif,fc->sci', normed_f, right_weight.astype(jnp.float32)) * coverage[:, None, :]).astype(jnp.bfloat16)
    count = jnp.dot(coverage.T, coverage, precision=lax.Precision.HIGHEST)
    scaled = (pair_output_gradient.astype(jnp.float32) / jnp.maximum(count, 1.0)[:, :, None]).astype(jnp.bfloat16)
    left_f = left.astype(jnp.float32)
    right_f = right.astype(jnp.float32)
    out_f = output_weight.astype(jnp.float32)
    out_three = out_f.reshape(PROJECTION_SIZE, PROJECTION_SIZE, PAIR)

    def one_block(carry, block_index):
        out_acc, right_acc = carry
        first = block_index * BLOCK_RES
        scaled_block = lax.dynamic_slice_in_dim(scaled, first, BLOCK_RES, 0).astype(jnp.float32)
        left_block = lax.dynamic_slice_in_dim(left_f, first, BLOCK_RES, 2)
        proj_sum = rounded(jnp.einsum('sej,ijk->seik', right_f, scaled_block))
        out_acc = out_acc + jnp.einsum('sci,seik->cek', left_block, proj_sum)
        left_part = jnp.einsum('seik,cek->sci', proj_sum, out_three)
        expanded = rounded(jnp.einsum('ijk,xk->ijx', scaled_block, out_f)).reshape(BLOCK_RES, RESIDUE_COUNT, PROJECTION_SIZE, PROJECTION_SIZE)
        right_acc = right_acc + jnp.einsum('sci,ijce->sej', left_block, expanded)
        return ((out_acc, right_acc), left_part)
    initial = (jnp.zeros((PROJECTION_SIZE, PROJECTION_SIZE, PAIR), jnp.float32), jnp.zeros((SEQUENCE_COUNT, PROJECTION_SIZE, RESIDUE_COUNT), jnp.float32))
    blocks = jnp.arange(RESIDUE_COUNT // BLOCK_RES, dtype=jnp.int32)
    (out_acc, right_acc), left_parts = lax.scan(one_block, initial, blocks)
    left_sum = jnp.transpose(left_parts, (1, 2, 0, 3)).reshape(SEQUENCE_COUNT, PROJECTION_SIZE, RESIDUE_COUNT)
    left_back = rounded(left_sum * coverage[:, None, :])
    right_back = rounded(right_acc * coverage[:, None, :])
    normed_grad = jnp.einsum('sci,fc->sif', left_back, left_weight.astype(jnp.float32))
    normed_grad = normed_grad + jnp.einsum('sci,fc->sif', right_back, right_weight.astype(jnp.float32))
    left_weight_gradient = jnp.einsum('sif,sci->fc', normed_f, left_back)
    right_weight_gradient = jnp.einsum('sif,sci->fc', normed_f, right_back)
    norm_gain_gradient = lax.optimization_barrier(jnp.sum(normed_grad * single_entry, axis=(0, 1)))
    norm_bias_gradient = lax.optimization_barrier(jnp.sum(normed_grad, axis=(0, 1)))
    rescaled_gradient = normed_grad * norm_gain_vector
    alignment_gradient = inverse_deviation * (rescaled_gradient - lax.optimization_barrier(jnp.mean(rescaled_gradient, axis=-1, keepdims=True)) - single_entry * lax.optimization_barrier(jnp.mean(rescaled_gradient * single_entry, axis=-1, keepdims=True)))
    output_weight_gradient = out_acc.reshape(PROJECTION_SIZE * PROJECTION_SIZE, PAIR)
    return (alignment_gradient.astype(jnp.bfloat16), norm_gain_gradient, norm_bias_gradient, left_weight_gradient, right_weight_gradient, output_weight_gradient)
```

```python
import functools

import jax
import jax.numpy as jnp
from jax import lax
from jax.experimental import pallas as pl
from jax.experimental.pallas import tpu as pltpu
from jax.sharding import PartitionSpec as P

CHAINS = 4
EPSILON = 1e-05
AXIS = "dap"
F32 = jnp.float32
BF16 = jnp.bfloat16
VMEM_LIMIT = 56 * 1024 * 1024


def mm(a, b, dims=(1, 0)):
    return lax.dot_general(
        a, b, (((dims[0],), (dims[1],)), ((), ())), preferred_element_type=F32
    )


def params(**more):
    return pltpu.CompilerParams(vmem_limit_bytes=VMEM_LIMIT, **more)


def whole(*shape):
    return pl.BlockSpec(shape, lambda *_: (0,) * len(shape))


def normalise(x):
    center = x - jnp.mean(x, axis=-1, keepdims=True)
    inverse = lax.rsqrt(jnp.mean(center * center, axis=-1, keepdims=True) + EPSILON)
    return center * inverse, inverse


def project_kernel(mask_ref, chain_ref, x_ref, gain_ref, bias_ref, lw_ref, rwt_ref,
                   rmask_ref, rchain_ref, left_ref, right_ref):
    me = lax.axis_index(AXIS)
    unit, _ = normalise(x_ref[...].astype(F32))
    normed = (unit * gain_ref[...] + bias_ref[...]).astype(BF16)
    left_ref[...] = mm(normed, lw_ref[...]).astype(BF16)
    chain = chain_ref[me]
    covered = jnp.logical_or(chain == CHAINS, rchain_ref[...] == chain)
    cover = jnp.where(covered, 1.0, 0.0) * (rmask_ref[...] * mask_ref[me]).astype(F32)
    right_ref[...] = (mm(rwt_ref[...], normed, (1, 1)) * cover).astype(BF16)


def project(x, gain, bias, lw, rwt, smask, schain, rmask, rchain):
    rows, _ = x.shape
    width = lw.shape[1]
    smem = pl.BlockSpec(memory_space=pltpu.SMEM)
    vmem = pl.BlockSpec(memory_space=pltpu.VMEM)
    return pl.pallas_call(
        project_kernel,
        out_shape=(
            jax.ShapeDtypeStruct((rows, width), BF16),
            jax.ShapeDtypeStruct((width, rows), BF16),
        ),
        in_specs=[smem, smem] + [vmem] * 7,
        out_specs=(vmem, vmem),
        compiler_params=params(),
        name="project",
    )(smask, schain, x, gain, bias, lw, rwt, rmask, rchain)


def scale_kernel(block, g_ref, r_ref, out_ref):
    pair = g_ref.shape[2]
    factor = jnp.transpose(r_ref[...])
    for b in range(block):
        out_ref[:, b * pair : (b + 1) * pair] = (
            g_ref[b].astype(F32) * factor[:, b : b + 1]
        ).astype(BF16)


def scale(gradient, reciprocal, block):
    rows, cols, pair = gradient.shape
    return pl.pallas_call(
        functools.partial(scale_kernel, block),
        grid=(rows // block,),
        out_shape=jax.ShapeDtypeStruct((cols, rows * pair), BF16),
        in_specs=[
            pl.BlockSpec((block, cols, pair), lambda b: (b, 0, 0)),
            pl.BlockSpec((block, cols), lambda b: (b, 0)),
        ],
        out_specs=pl.BlockSpec((cols, block * pair), lambda b: (0, b)),
        compiler_params=params(),
        cost_estimate=pl.CostEstimate(
            flops=gradient.size, bytes_accessed=4 * gradient.size, transcendentals=0
        ),
        name="scale",
    )(gradient, reciprocal)


def order_left(l_ref, scratch):
    seqs, rows, _ = l_ref.shape
    for s in range(seqs):
        scratch[pl.ds(s, rows, stride=seqs), :] = l_ref[s].astype(F32)


def left_block(scratch, mask_ref, step, size):
    at = pl.ds(pl.multiple_of(step * size, size), size)
    return (scratch[at, :] * mask_ref[at, :]).astype(BF16)


def right_sum_kernel(block, l_ref, mask_ref, w_ref, s_ref, out_ref, ordered, mixed, total):
    step = pl.program_id(0)
    seqs = l_ref.shape[0]
    pair = s_ref.shape[1] // block
    width = w_ref.shape[1] // pair

    @pl.when(step == 0)
    def _():
        order_left(l_ref, ordered)
        total[...] = jnp.zeros_like(total)

    left = left_block(ordered, mask_ref, step, block * seqs)
    group = 8
    for first in range(0, width, group):
        part = mm(left, w_ref[:, first * pair : (first + group) * pair]).astype(BF16)
        for e in range(group):
            for i in range(block):
                mixed[(first + e) * seqs : (first + e + 1) * seqs, i * pair : (i + 1) * pair] = part[
                    i * seqs : (i + 1) * seqs, e * pair : (e + 1) * pair
                ]
    total[...] += mm(s_ref[...], mixed[...], (1, 1))

    @pl.when(step == pl.num_programs(0) - 1)
    def _():
        out_ref[...] = total[...].astype(BF16)


def right_sum(left, mask, weight, scaled, block):
    seqs, rows, width = left.shape
    cols = scaled.shape[0]
    pair = scaled.shape[1] // rows
    wide = weight.shape[1] // pair * seqs
    return pl.pallas_call(
        functools.partial(right_sum_kernel, block),
        grid=(rows // block,),
        out_shape=jax.ShapeDtypeStruct((cols, wide), BF16),
        in_specs=[
            whole(*left.shape),
            whole(*mask.shape),
            whole(*weight.shape),
            pl.BlockSpec((cols, block * pair), lambda b: (0, b)),
        ],
        out_specs=whole(cols, wide),
        scratch_shapes=[
            pltpu.VMEM((rows * seqs, width), F32),
            pltpu.VMEM((wide, block * pair), BF16),
            pltpu.VMEM((cols, wide), F32),
        ],
        compiler_params=params(),
        cost_estimate=pl.CostEstimate(
            flops=2 * cols * wide * rows * pair, bytes_accessed=2 * scaled.size, transcendentals=0
        ),
        name="right_sum",
    )(left, mask, weight, scaled)


def left_side_kernel(block, sorting, *refs):
    if sorting:
        near_ref, far_ref, sort_ref, *refs = refs
        l_ref, mask_ref, w_ref, s_ref, back_ref, out_ref, ordered, proj, total, spread, right = refs
    else:
        right, *refs = refs
        l_ref, mask_ref, w_ref, s_ref, back_ref, out_ref, ordered, proj, total, spread = refs
    step = pl.program_id(0)
    seqs = l_ref.shape[0]
    pair = s_ref.shape[1] // block
    width = w_ref.shape[0] // pair

    @pl.when(step == 0)
    def _():
        order_left(l_ref, ordered)
        total[...] = jnp.zeros_like(total)
        if sorting:
            half = near_ref.shape[0]
            right[...] = (
                mm(sort_ref[:, :half], near_ref[...]) + mm(sort_ref[:, half:], far_ref[...])
            ).astype(BF16)

    for i in range(block):
        part = mm(right[...], s_ref[:, i * pair : (i + 1) * pair]).astype(BF16)
        for e in range(width):
            proj[i * seqs : (i + 1) * seqs, e * pair : (e + 1) * pair] = part[
                e * seqs : (e + 1) * seqs, :
            ]
    left = left_block(ordered, mask_ref, step, block * seqs)
    back_ref[...] = mm(proj[...], w_ref[...])
    total[...] += mm(left, proj[...], (0, 0))

    @pl.when(step == pl.num_programs(0) - 1)
    def _():
        for e in range(width):
            spread[pl.ds(e, total.shape[0], stride=width), :] = total[:, e * pair : (e + 1) * pair]
        out_ref[...] = spread[...].astype(BF16)


def left_side(rights, left, mask, weight, scaled, block):
    seqs, rows, width = left.shape
    cols = scaled.shape[0]
    pair = scaled.shape[1] // rows
    return pl.pallas_call(
        functools.partial(left_side_kernel, block, len(rights) > 1),
        grid=(rows // block,),
        out_shape=(
            jax.ShapeDtypeStruct((rows * seqs, width), F32),
            jax.ShapeDtypeStruct((width * width, pair), BF16),
        ),
        in_specs=[whole(*a.shape) for a in rights]
        + [
            whole(*left.shape),
            whole(*mask.shape),
            whole(*weight.shape),
            pl.BlockSpec((cols, block * pair), lambda b: (0, b)),
        ],
        out_specs=(
            pl.BlockSpec((block * seqs, width), lambda b: (b, 0)),
            whole(width * width, pair),
        ),
        scratch_shapes=[
            pltpu.VMEM((rows * seqs, width), F32),
            pltpu.VMEM((block * seqs, width * pair), BF16),
            pltpu.VMEM((width, width * pair), F32),
            pltpu.VMEM((width * width, pair), F32),
        ]
        + [pltpu.VMEM((width * seqs, cols), BF16)] * (len(rights) > 1),
        compiler_params=params(),
        cost_estimate=pl.CostEstimate(
            flops=2 * cols * width * seqs * rows * pair,
            bytes_accessed=2 * scaled.size,
            transcendentals=0,
        ),
        name="left_side",
    )(*rights, left, mask, weight, scaled)


def owner_kernel(seqs, swapping, *refs):
    if swapping:
        swap_ref, *refs = refs
    (parts_ref, back_ref, lmask_ref, rmask_ref, x_ref, gain_ref, bias_ref, w_ref,
     sums_ref, home_ref, masked, rows_ref) = refs
    count, res, _ = parts_ref.shape
    width = back_ref.shape[1]
    right = parts_ref[0].astype(F32)
    for p in range(1, count):
        right = right + parts_ref[p].astype(F32)
    right = (right * rmask_ref[...]).astype(BF16)
    right = mm(right, swap_ref[...]) if swapping else right.astype(F32)
    masked[...] = back_ref[...] * lmask_ref[...]
    for s in range(seqs):
        rows_ref[s * res : (s + 1) * res, :width] = masked[pl.ds(s, res, stride=seqs), :]
        rows_ref[s * res : (s + 1) * res, width:] = right[:, s * width : (s + 1) * width]
    both = rows_ref[...].astype(BF16)
    home_ref[...] = both
    unit, _ = normalise(x_ref[...].astype(F32))
    normed = (unit * gain_ref[...] + bias_ref[...]).astype(BF16)
    normed_grad = mm(both, w_ref[...], (1, 1))
    sums_ref[: 2 * width, :] = mm(both, normed, (0, 0))
    sums_ref[2 * width : 2 * width + 1, :] = jnp.sum(normed_grad * unit, axis=0, keepdims=True)
    sums_ref[2 * width + 1 : 2 * width + 2, :] = jnp.sum(normed_grad, axis=0, keepdims=True)
    sums_ref[2 * width + 2 :, :] = jnp.zeros((6, sums_ref.shape[1]), F32)


def owner(swap, parts, back, lmask, rmask, x, gain, bias, weights, seqs):
    rows, width = back.shape
    features = x.shape[1]
    vmem = pl.BlockSpec(memory_space=pltpu.VMEM)
    return pl.pallas_call(
        functools.partial(owner_kernel, seqs, bool(swap)),
        out_shape=(
            jax.ShapeDtypeStruct((2 * width + 8, features), F32),
            jax.ShapeDtypeStruct((rows, 2 * width), BF16),
        ),
        in_specs=[vmem] * (8 + len(swap)),
        out_specs=(vmem, vmem),
        scratch_shapes=[pltpu.VMEM((rows, width), F32), pltpu.VMEM((rows, 2 * width), F32)],
        compiler_params=params(),
        name="owner",
    )(*swap, parts, back, lmask, rmask, x, gain, bias, weights)


def home_kernel(both_ref, x_ref, gain_ref, w_ref, out_ref):
    unit, inverse = normalise(x_ref[...].astype(F32))
    d = mm(both_ref[...], w_ref[...], (1, 1)) * gain_ref[...]
    out_ref[...] = (
        inverse
        * (
            d
            - jnp.mean(d, axis=-1, keepdims=True)
            - unit * jnp.mean(d * unit, axis=-1, keepdims=True)
        )
    ).astype(BF16)


def home(both, x, gain, weights):
    vmem = pl.BlockSpec(memory_space=pltpu.VMEM)
    return pl.pallas_call(
        home_kernel,
        out_shape=jax.ShapeDtypeStruct(x.shape, BF16),
        in_specs=[vmem] * 4,
        out_specs=vmem,
        compiler_params=params(),
        name="home",
    )(both, x, gain, weights)


def on_device(
    size,
    alignment_rows,
    norm_gain_vector,
    norm_bias_vector,
    left_weight,
    right_weight,
    output_weight,
    pair_output_gradient,
    sequence_real_mask,
    sequence_chain_index,
    residue_real_mask,
    residue_chain_index,
):
    me = lax.axis_index(AXIS)
    core = me % 2
    chips = size // 2
    same_core = [[d for d in range(size) if d % 2 == c] for c in (0, 1)]
    res, cols, pair = pair_output_gradient.shape
    width = left_weight.shape[1]
    features = left_weight.shape[0]
    seqs = sequence_real_mask.shape[0]
    block = max(b for b in range(1, 9) if res % b == 0)

    def swap_with(value, bit):
        return lax.ppermute(value, AXIS, [(d, d ^ bit) for d in range(size)])

    x = alignment_rows.reshape(cols, features)
    gain = norm_gain_vector.reshape(1, features)
    bias = norm_bias_vector.reshape(1, features)
    left, right = project(
        x, gain, bias, left_weight, right_weight.T,
        sequence_real_mask, sequence_chain_index,
        residue_real_mask.reshape(1, cols), residue_chain_index.reshape(1, cols),
    )
    left_all = lax.all_to_all(left.reshape(size, res, width), AXIS, 0, 0, tiled=True)
    near = lax.all_to_all(
        jnp.broadcast_to(right, (chips, width, cols)), AXIS, 0, 0, tiled=True,
        axis_index_groups=same_core,
    ).reshape(chips * width, cols)
    far = swap_with(near, 1)
    x_own = lax.all_to_all(x.reshape(size, res, features), AXIS, 0, 0, tiled=True)
    x_own = x_own.reshape(size * res, features)

    covered = (sequence_chain_index[:, None] == CHAINS) | (
        sequence_chain_index[:, None] == residue_chain_index[None, :]
    )
    coverage = (
        jnp.where(covered, 1.0, 0.0)
        * sequence_real_mask[:, None].astype(F32)
        * residue_real_mask[None, :].astype(F32)
    )
    own = lax.dynamic_slice_in_dim(coverage, me * res, res, 1)
    count = mm(own.astype(BF16), coverage.astype(BF16), (0, 0))
    reciprocal = 1.0 / jnp.maximum(count, 1.0)
    lmask = own.T.reshape(res * seqs, 1)
    rmask = jnp.tile(own.T, (1, width))

    def place(n, dim):
        return lax.broadcasted_iota(jnp.int32, (n, n), dim)

    wide = width * seqs
    small = wide <= 1024
    if small:
        row, col = place(wide, 0), place(wide, 1)
        from_core, chip, at = col // (chips * width), (col // width) % chips, col % width
        sort = (row == at * seqs + 2 * chip + (from_core ^ core)).astype(BF16)
        rights = [near, far, sort]
        swap = [((row // seqs == col % width) & (row % seqs == col // width)).astype(BF16)]
    else:
        even, odd = jnp.where(core == 0, near, far), jnp.where(core == 0, far, near)
        both = jnp.stack([even.reshape(chips, width, cols), odd.reshape(chips, width, cols)])
        rights = [both.transpose(2, 1, 0, 3).reshape(wide, cols)]
        swap = []

    w_mix = output_weight.reshape(width, width * pair)
    w_back = w_mix.T
    weights = jnp.concatenate([left_weight, right_weight], axis=1)

    scaled = scale(pair_output_gradient, reciprocal, block)
    shares = right_sum(left_all, lmask, w_mix, scaled, block).reshape(chips, 2, res, wide)
    keep = lax.dynamic_index_in_dim(shares, core, 1, keepdims=False)
    give = lax.dynamic_index_in_dim(shares, 1 - core, 1, keepdims=False)
    of_chip = (keep.astype(F32) + swap_with(give, 1).astype(F32)).astype(BF16)
    parts = lax.all_to_all(of_chip, AXIS, 0, 0, tiled=True, axis_index_groups=same_core)

    back, out_share = left_side(rights, left_all, lmask, w_back, scaled, block)
    out_parts = lax.all_to_all(
        out_share.reshape(size, width * width // size, pair), AXIS, 0, 0, tiled=True
    )
    out_piece = jnp.sum(out_parts.astype(F32), axis=0).astype(BF16)[None]

    if not small:
        parts = jnp.sum(parts.astype(F32), axis=0, keepdims=True)
        parts = parts.reshape(1, res, width, seqs).swapaxes(2, 3).reshape(1, res, wide)
        rmask = jnp.repeat(own.T, width, axis=1)
    sums, both = owner(swap, parts, back, lmask, rmask, x_own, gain, bias, weights, seqs)
    both_home = lax.all_to_all(both.reshape(size, res, 2 * width), AXIS, 0, 0, tiled=True)

    bit = size // 2
    while bit:
        sums = sums + swap_with(sums, bit)
        out_piece = jnp.concatenate([out_piece, swap_with(out_piece, bit)], axis=0)
        bit //= 2
    bits = size.bit_length() - 1
    wanted = jnp.arange(size) ^ me
    spot = sum(((wanted >> b) & 1) << (bits - 1 - b) for b in range(bits))
    out_weight_gradient = jnp.take(out_piece, spot, axis=0).astype(F32).reshape(width * width, pair)

    alignment_gradient = home(both_home.reshape(cols, 2 * width), x, gain, weights)
    return (
        alignment_gradient.reshape(alignment_rows.shape),
        sums[2 * width],
        sums[2 * width + 1],
        sums[:width].T,
        sums[width : 2 * width].T,
        out_weight_gradient,
    )


def solution(mesh):
    rows = P(("grp", "dap"), None, None)
    in_specs = (rows, P(), P(), P(), P(), P(), rows, P("grp"), P("grp"), P("grp"), P("grp"))
    out_specs = (rows, P("grp"), P("grp"), P("grp", None), P("grp", None), P("grp", None))
    return jax.shard_map(
        functools.partial(on_device, mesh.shape[AXIS]),
        mesh=mesh,
        in_specs=in_specs,
        out_specs=out_specs,
        check_vma=False,
    )
```

```python
import functools

import jax
import jax.numpy as jnp
from jax import lax
from jax.experimental import pallas as pl
from jax.experimental.pallas import tpu as pltpu
from jax.sharding import PartitionSpec as P

CHAINS = 4
EPSILON = 1e-05
AXIS = "dap"
F32 = jnp.float32
BF16 = jnp.bfloat16
LANES = 128
MIB = 1024 * 1024
VMEM = pl.BlockSpec(memory_space=pltpu.VMEM)


def mm(a, b, dims=(1, 0)):
    return lax.dot_general(
        a, b, (((dims[0],), (dims[1],)), ((), ())), preferred_element_type=F32
    )


def in_hbm(value):
    return pltpu.with_memory_space_constraint(value, pltpu.HBM)


def params(mib):
    return pltpu.CompilerParams(vmem_limit_bytes=mib * MIB)


def whole(*shape):
    return pl.BlockSpec(shape, lambda *_: (0,) * len(shape))


def sds(shape, dtype):
    return jax.ShapeDtypeStruct(shape, dtype)


def up(n, to=16):
    return -(-n // to) * to


class Sizes:
    def __init__(self, size, res, cols, pair, width, features, seqs):
        self.size, self.res, self.cols, self.pair = size, res, cols, pair
        self.width, self.features, self.seqs = width, features, seqs
        self.chips = size // 2
        self.planes = cols // LANES
        self.wide = width * seqs
        self.groups = max(g for g in (4, 3, 2, 1) if g == 1 or res % (16 * g) == 0)
        self.rows = res // self.groups
        self.slots = up(self.rows)
        self.piece = width * width // size
        self.piece_slots = up(self.piece)
        self.sum_rows = up(2 * width + 2, 8) * features // LANES
        self.block = max(b for b in range(1, 9) if res % b == 0)
        blocks = res // self.block
        self.pieces = max(n for n in (3, 2, 1) if blocks % n == 0)
        self.per_piece = blocks // self.pieces
        self.mib = 28 if self.wide <= 1024 else 56
        bits = size.bit_length() - 1
        self.masks = [size >> (b + 1) for b in range(bits)]

    def origin(self, p):
        return sum(m * ((p >> b) & 1) for b, m in enumerate(self.masks))


def normalise(x):
    center = x - jnp.mean(x, axis=-1, keepdims=True)
    inverse = lax.rsqrt(jnp.mean(center * center, axis=-1, keepdims=True) + EPSILON)
    return center * inverse, inverse


def project_kernel(z, x_ref, gain_ref, bias_ref, lwt_ref, rwt_ref,
                   left_ref, right_ref, unit_ref, inverse_ref):
    unit, inverse = normalise(x_ref[...].astype(F32))
    normed = (unit * gain_ref[...] + bias_ref[...]).astype(BF16)
    right_ref[...] = mm(rwt_ref[...], normed, (1, 1)).astype(BF16)
    left = mm(normed, lwt_ref[...], (1, 1))
    for d in range(z.size):
        parts = [
            left[d * z.res + g * z.rows : d * z.res + (g + 1) * z.rows] for g in range(z.groups)
        ]
        parts.append(jnp.zeros((z.rows, LANES - z.groups * z.width), F32))
        packed = jnp.concatenate(parts, axis=1)
        if z.slots > z.rows:
            packed = jnp.concatenate([packed, jnp.zeros((z.slots - z.rows, LANES), F32)], axis=0)
        left_ref[d] = packed.astype(BF16)
    unit_ref[...] = unit
    inverse_ref[...] = inverse


def project(z, x, gain, bias, lwt, rwt):
    return pl.pallas_call(
        functools.partial(project_kernel, z),
        out_shape=(
            sds((z.size, z.slots, LANES), BF16),
            sds((z.width, z.cols), BF16),
            sds((z.cols, z.features), F32),
            sds((z.cols, 1), F32),
        ),
        in_specs=[VMEM] * 5,
        out_specs=(VMEM,) * 4,
        compiler_params=params(16),
        name="project",
    )(x, gain, bias, lwt, rwt)


def cover_kernel(z, smask_ref, schain_ref, code_ref, w_ref, cover_ref, own_ref, mine_ref, mix_ref,
                 rows):
    me = lax.axis_index(AXIS)
    code = code_ref[...]
    real = (code >= 8).astype(F32)
    chain = code % 8

    def covered(s):
        same = jnp.logical_or(schain_ref[s] == CHAINS, chain == schain_ref[s])
        return jnp.where(same, real * smask_ref[s].astype(F32), 0.0)

    for s in range(z.seqs):
        cover_ref[s : s + 1, :] = covered(s)
    mine_ref[...] = covered(me)
    turned = pltpu.roll(cover_ref[...], z.cols - me * z.res, 1)
    own_ref[...] = jnp.transpose(turned[:, :LANES])[: z.res, :]
    rows[...] = w_ref[...].astype(F32)
    for e in range(z.width):
        part = rows[pl.ds(e, z.width, stride=z.width), :]
        mix_ref[:, e * z.pair : (e + 1) * z.pair] = part.astype(BF16)


def cover_all(z, smask, schain, code, weight):
    smem = pl.BlockSpec(memory_space=pltpu.SMEM)
    return pl.pallas_call(
        functools.partial(cover_kernel, z),
        out_shape=(
            sds((z.seqs, z.cols), F32),
            sds((z.res, z.seqs), F32),
            sds((1, z.cols), F32),
            sds((z.width, z.width * z.pair), BF16),
        ),
        in_specs=[smem, smem, VMEM, VMEM],
        out_specs=(VMEM,) * 4,
        scratch_shapes=[pltpu.VMEM(weight.shape, F32)],
        compiler_params=params(8),
        name="cover",
    )(smask, schain, code, in_hbm(weight))


def scale_kernel(z, g_ref, own_ref, cover_ref, out_ref):
    block, pair = z.block, z.pair
    count = mm(own_ref[0].astype(BF16), cover_ref[...].astype(BF16))
    factor = 1.0 / jnp.maximum(count, 1.0)
    high = factor.astype(BF16)
    low = (factor - high.astype(F32)).astype(BF16)
    shape = (block, block * pair)
    pick = (
        lax.broadcasted_iota(jnp.int32, shape, 0)
        == lax.broadcasted_iota(jnp.int32, shape, 1) // pair
    ).astype(F32).astype(BF16)
    spread = mm(high, pick, (0, 0)) + mm(low, pick, (0, 0))
    for b in range(block):
        at = slice(b * pair, (b + 1) * pair)
        out_ref[:, at] = (g_ref[b].astype(F32) * spread[:, at]).astype(BF16)


def scale(z, gradient, own, cover, piece):
    steps = z.per_piece
    size = gradient.size // z.pieces
    return pl.pallas_call(
        functools.partial(scale_kernel, z),
        grid=(steps,),
        out_shape=pltpu.HBM((z.cols, steps * z.block * z.pair), BF16),
        in_specs=[
            pl.BlockSpec((z.block, z.cols, z.pair), lambda b: (piece * steps + b, 0, 0)),
            pl.BlockSpec((1, z.block, z.seqs), lambda b: (piece * steps + b, 0, 0)),
            whole(*cover.shape),
        ],
        out_specs=pl.BlockSpec((z.cols, z.block * z.pair), lambda b: (0, b)),
        compiler_params=params(20),
        cost_estimate=pl.CostEstimate(flops=size, bytes_accessed=4 * size, transcendentals=0),
        name="scale",
    )(in_hbm(gradient), own.reshape(z.res // z.block, z.block, z.seqs), cover)


def order_left(z, l_ref, own_ref, scratch):
    for s in range(z.seqs):
        got = l_ref[s].astype(F32)
        for g in range(z.groups):
            at = slice(g * z.rows, (g + 1) * z.rows)
            part = got[: z.rows, g * z.width : (g + 1) * z.width] * own_ref[at, s : s + 1]
            scratch[pl.ds(g * z.rows * z.seqs + s, z.rows, stride=z.seqs), :] = part


def scaled_copy(z, s_refs, here, arrived, piece, step):
    size = z.block * z.pair
    at = piece * z.per_piece + step
    source = pl.ds(pl.multiple_of(step * size, size), size)
    span = pl.ds(pl.multiple_of(at * size, size), size)
    return pltpu.make_async_copy(s_refs[piece].at[:, source], here.at[:, span], arrived.at[at]), span


def fetch_scaled(z, s_refs, here, arrived):
    for piece in range(z.pieces):
        for step in range(z.per_piece):
            scaled_copy(z, s_refs, here, arrived, piece, step)[0].start()


def over_scaled(z, s_refs, here, arrived, body):
    for piece in range(z.pieces):

        @pl.loop(0, z.per_piece)
        def _(step):
            copy, span = scaled_copy(z, s_refs, here, arrived, piece, step)
            copy.wait()
            body(piece * z.per_piece + step, span)


def right_sum_kernel(z, l_ref, own_ref, w_ref, *refs):
    s_refs = refs[: z.pieces]
    keep_ref, give_ref, ordered, mixed, total, here, arrived = refs[z.pieces :]
    core = lax.axis_index(AXIS) % 2
    seqs, pair = z.seqs, z.pair
    fetch_scaled(z, s_refs, here, arrived)
    order_left(z, l_ref, own_ref, ordered)
    left = ordered[...].astype(BF16)
    group = 8
    for first in range(0, z.width, group):
        part = mm(left, w_ref[:, first * pair : (first + group) * pair]).astype(BF16)
        for e in range(group):
            for i in range(z.res):
                mixed[(first + e) * seqs : (first + e + 1) * seqs, i * pair : (i + 1) * pair] = part[
                    i * seqs : (i + 1) * seqs, e * pair : (e + 1) * pair
                ]

    total[...] = jnp.zeros_like(total)

    def add(_, span):
        product = mm(mixed[:, span], here[:, span], (1, 1))
        for c in range(z.planes):
            total[c] += product[:, c * LANES : (c + 1) * LANES]

    over_scaled(z, s_refs, here, arrived, add)
    for chip in range(z.chips):
        for ref, parity in ((keep_ref, core), (give_ref, 1 - core)):
            at = pl.ds(2 * chip + parity, z.width, stride=seqs)
            for c in range(z.planes):
                ref[chip, :, c * LANES : (c + 1) * LANES] = total[c, at, :].astype(BF16)


def right_sum(z, left, own, weight, scaled):
    out = (z.chips, z.width, z.cols)
    return pl.pallas_call(
        functools.partial(right_sum_kernel, z),
        out_shape=(sds(out, BF16), sds(out, BF16)),
        in_specs=[VMEM] * 3 + [pl.BlockSpec(memory_space=pltpu.HBM)] * z.pieces,
        out_specs=(VMEM, VMEM),
        scratch_shapes=[
            pltpu.VMEM((z.res * z.seqs, z.width), F32),
            pltpu.VMEM((z.wide, z.res * z.pair), BF16),
            pltpu.VMEM((z.planes, z.wide, LANES), F32),
            pltpu.VMEM((z.cols, z.res * z.pair), BF16),
            pltpu.SemaphoreType.DMA((z.res // z.block,)),
        ],
        compiler_params=params(z.mib),
        cost_estimate=pl.CostEstimate(
            flops=2 * z.wide * z.cols * z.res * z.pair, bytes_accessed=0, transcendentals=0
        ),
        name="right_sum",
    )(left, own, weight, *[in_hbm(piece) for piece in scaled])


def left_side_kernel(z, here_ref, there_ref, cover_ref, l_ref, own_ref, w_ref, *refs):
    s_refs = refs[: z.pieces]
    out_ref, ordered, right, proj, back, wide_rows, here, arrived = refs[z.pieces :]
    me = lax.axis_index(AXIS)
    seqs, pair, block, width = z.seqs, z.pair, z.block, z.width
    fetch_scaled(z, s_refs, here, arrived)
    order_left(z, l_ref, own_ref, ordered)
    for side, ref in ((0, here_ref), (z.size // 2, there_ref)):

        @pl.loop(0, z.size // 2)
        def _(p):
            at = pl.ds(me ^ z.origin(p + side), width, stride=seqs)
            for c in range(z.planes):
                wide_rows[c, at, :] = ref[p, :, c * LANES : (c + 1) * LANES].astype(F32)

    for e in range(width):
        at = slice(e * seqs, (e + 1) * seqs)
        for c in range(z.planes):
            lanes = slice(c * LANES, (c + 1) * LANES)
            right[at, lanes] = (wide_rows[c, at, :] * cover_ref[:, lanes]).astype(BF16)

    def project_block(step, span):
        group = width // 4
        for first in range(0, width, group):
            part = mm(right[first * seqs : (first + group) * seqs, :], here[:, span])
            part = part.astype(BF16)
            for i in range(block):
                at = pl.ds(pl.multiple_of((step * block + i) * seqs, seqs), seqs)
                for e in range(group):
                    proj[at, (first + e) * pair : (first + e + 1) * pair] = part[
                        e * seqs : (e + 1) * seqs, i * pair : (i + 1) * pair
                    ]

    over_scaled(z, s_refs, here, arrived, project_block)
    back[...] = mm(proj[...], w_ref[...], (1, 1))
    spread = wide_rows.at[0]
    left = ordered[...].astype(BF16)
    for first in range(0, width, 8):
        total = mm(left, proj[:, first * pair : (first + 8) * pair], (0, 0))
        for e in range(8):
            spread[pl.ds(first + e, width, stride=width), :] = total[:, e * pair : (e + 1) * pair]
    for d in range(z.size):
        got = spread[d * z.piece : (d + 1) * z.piece, :]
        if z.piece_slots > z.piece:
            got = jnp.concatenate([got, jnp.zeros((z.piece_slots - z.piece, pair), F32)], axis=0)
        out_ref[d, : z.piece_slots] = got.astype(BF16)
        parts = [
            back[pl.ds(g * z.rows * seqs + d, z.rows, stride=seqs), :] for g in range(z.groups)
        ]
        parts.append(jnp.zeros((z.rows, LANES - z.groups * width), F32))
        packed = jnp.concatenate(parts, axis=1)
        if z.slots > z.rows:
            packed = jnp.concatenate([packed, jnp.zeros((z.slots - z.rows, LANES), F32)], axis=0)
        out_ref[d, z.piece_slots :] = packed.astype(BF16)


def left_side(z, here, there, cover, left, own, weight, scaled):
    return pl.pallas_call(
        functools.partial(left_side_kernel, z),
        out_shape=sds((z.size, z.piece_slots + z.slots, LANES), BF16),
        in_specs=[VMEM] * 6 + [pl.BlockSpec(memory_space=pltpu.HBM)] * z.pieces,
        out_specs=VMEM,
        scratch_shapes=[
            pltpu.VMEM((z.res * z.seqs, z.width), F32),
            pltpu.VMEM((z.wide, z.cols), BF16),
            pltpu.VMEM((z.res * z.seqs, z.width * z.pair), BF16),
            pltpu.VMEM((z.res * z.seqs, z.width), F32),
            pltpu.VMEM((z.planes, max(z.wide, z.width * z.width), LANES), F32),
            pltpu.VMEM((z.cols, z.res * z.pair), BF16),
            pltpu.SemaphoreType.DMA((z.res // z.block,)),
        ],
        compiler_params=params(z.mib),
        cost_estimate=pl.CostEstimate(
            flops=2 * z.wide * z.cols * z.res * z.pair, bytes_accessed=0, transcendentals=0
        ),
        name="left_side",
    )(here, there, cover, left, own, weight, *[in_hbm(piece) for piece in scaled])


def owner_kernel(z, parts_ref, got_ref, cover_ref, unit_ref, gain_ref, bias_ref, lwt_ref, rwt_ref,
                 sums_ref, grad_ref, rows):
    width = z.width
    cover = cover_ref[...]
    right = parts_ref[0].astype(F32)
    for p in range(1, z.chips):
        right = right + parts_ref[p].astype(F32)
    right = (right * cover).astype(BF16)
    piece = got_ref[0, : z.piece_slots].astype(F32)
    for d in range(1, z.size):
        piece = piece + got_ref[d, : z.piece_slots].astype(F32)
    for d in range(z.size):
        got = got_ref[d, z.piece_slots :].astype(F32)
        for g in range(z.groups):
            first = d * z.res + g * z.rows
            rows[first : first + z.rows, :] = got[: z.rows, g * width : (g + 1) * width]
    column = jnp.transpose(jnp.broadcast_to(cover, (8, z.cols)))[:, :1]
    left = (rows[...] * column).astype(BF16)
    unit = unit_ref[...]
    normed = (unit * gain_ref[...] + bias_ref[...]).astype(BF16)
    grad = mm(left, lwt_ref[...]) + mm(right, rwt_ref[...], (0, 0))
    grad_ref[...] = grad
    pad = up(2 * width + 2, 8) - 2 * width - 2
    sums = jnp.concatenate(
        [
            mm(left, normed, (0, 0)),
            mm(right, normed),
            jnp.sum(grad * unit, axis=0, keepdims=True),
            jnp.sum(grad, axis=0, keepdims=True),
            jnp.zeros((pad, z.features), F32),
        ],
        axis=0,
    )
    half = sums.shape[0]
    for part in range(z.features // LANES):
        sums_ref[part * half : (part + 1) * half, :] = sums[
            :, part * LANES : (part + 1) * LANES
        ].astype(BF16)
    sums_ref[z.sum_rows :, :] = piece.astype(BF16)


def owner(z, parts, got, cover, unit, gain, bias, lwt, rwt):
    return pl.pallas_call(
        functools.partial(owner_kernel, z),
        out_shape=(
            sds((z.sum_rows + z.piece_slots, LANES), BF16),
            sds((z.cols, z.features), F32),
        ),
        in_specs=[VMEM] * 8,
        out_specs=(VMEM, VMEM),
        scratch_shapes=[pltpu.VMEM((z.cols, z.width), F32)],
        compiler_params=params(24),
        name="owner",
    )(parts, got, cover, unit, gain, bias, lwt, rwt)


def stack_kernel(here_ref, there_ref, out_ref):
    half = here_ref.shape[0]
    out_ref[:half] = here_ref[...]
    out_ref[half:] = there_ref[...]


def stack(here, there):
    return pl.pallas_call(
        stack_kernel,
        out_shape=sds((2 * here.shape[0],) + here.shape[1:], here.dtype),
        in_specs=[VMEM, VMEM],
        out_specs=VMEM,
        compiler_params=params(16),
        name="stack",
    )(here, there)


def pair_sum_kernel(here_ref, there_ref, out_ref):
    for p in range(here_ref.shape[0]):
        out_ref[p] = (here_ref[p].astype(F32) + there_ref[p].astype(F32)).astype(BF16)


def pair_sum(here, there):
    return pl.pallas_call(
        pair_sum_kernel,
        out_shape=sds(here.shape, BF16),
        in_specs=[VMEM, VMEM],
        out_specs=VMEM,
        compiler_params=params(24),
        name="pair_sum",
    )(here, there)


def join_kernel(z, here_ref, there_ref, out_ref):
    top, more = z.sum_rows, here_ref.shape[0] - z.sum_rows
    out_ref[:top, :] = (here_ref[:top, :].astype(F32) + there_ref[:top, :].astype(F32)).astype(BF16)
    out_ref[top : top + more, :] = here_ref[top:, :]
    out_ref[top + more :, :] = there_ref[top:, :]


def join(z, here, there):
    rows = 2 * here.shape[0] - z.sum_rows
    return pl.pallas_call(
        functools.partial(join_kernel, z),
        out_shape=sds((rows, LANES), BF16),
        in_specs=[VMEM, VMEM],
        out_specs=VMEM,
        compiler_params=params(8),
        name="join",
    )(here, there)


def finish_kernel(z, here_ref, there_ref, lw_ref, rw_ref, gain_ref, bias_ref, out_ref):
    me = lax.axis_index(AXIS)
    top, width = z.sum_rows, z.width
    sums = here_ref[:top, :].astype(F32) + there_ref[:top, :].astype(F32)
    half = top // (z.features // LANES)
    for part in range(z.features // LANES):
        at = slice(part * LANES, (part + 1) * LANES)
        lw_ref[:, at] = sums[part * half : part * half + width]
        rw_ref[:, at] = sums[part * half + width : part * half + 2 * width]
        gain_ref[:, at] = sums[part * half + 2 * width : part * half + 2 * width + 1]
        bias_ref[:, at] = sums[part * half + 2 * width + 1 : part * half + 2 * width + 2]
    for p in range(z.size):
        ref = here_ref if p < z.size // 2 else there_ref
        first = top + (p % (z.size // 2)) * z.piece_slots
        at = pl.ds(pl.multiple_of((me ^ z.origin(p)) * z.piece, z.piece), z.piece)
        out_ref[at, :] = ref[first : first + z.piece_slots, :].astype(F32)[: z.piece]


def finish(z, here, there):
    return pl.pallas_call(
        functools.partial(finish_kernel, z),
        out_shape=(
            sds((z.width, z.features), F32),
            sds((z.width, z.features), F32),
            sds((1, z.features), F32),
            sds((1, z.features), F32),
            sds((z.width * z.width, z.pair), F32),
        ),
        in_specs=[VMEM, VMEM],
        out_specs=(VMEM,) * 5,
        compiler_params=params(8),
        name="finish",
    )(here, there)


def home_kernel(grad_ref, unit_ref, inverse_ref, gain_ref, out_ref):
    unit = unit_ref[...]
    d = grad_ref[...] * gain_ref[...]
    out_ref[...] = (
        inverse_ref[...]
        * (
            d
            - jnp.mean(d, axis=-1, keepdims=True)
            - unit * jnp.mean(d * unit, axis=-1, keepdims=True)
        )
    ).astype(BF16)


def home(z, grad, unit, inverse, gain):
    return pl.pallas_call(
        home_kernel,
        out_shape=sds(unit.shape, BF16),
        in_specs=[VMEM] * 4,
        out_specs=VMEM,
        compiler_params=params(16),
        name="home",
    )(grad, unit, inverse, gain)


def on_device(
    size,
    alignment_rows,
    norm_gain_vector,
    norm_bias_vector,
    left_weight,
    right_weight,
    output_weight,
    pair_output_gradient,
    sequence_real_mask,
    sequence_chain_index,
    residue_real_mask,
    residue_chain_index,
):
    me = lax.axis_index(AXIS)
    res, cols, pair = pair_output_gradient.shape
    features, width = left_weight.shape
    seqs = sequence_real_mask.shape[0]
    z = Sizes(size, res, cols, pair, width, features, seqs)
    same_core = [[d for d in range(size) if d % 2 == c] for c in (0, 1)]

    def swap_with(value, bit):
        return lax.ppermute(value, AXIS, [(d, d ^ bit) for d in range(size)])

    x = alignment_rows.reshape(cols, features)
    gain = norm_gain_vector.reshape(1, features)
    bias = norm_bias_vector.reshape(1, features)
    lwt, rwt = left_weight.T, right_weight.T
    left, right, unit, inverse = project(
        z, in_hbm(x), in_hbm(gain), in_hbm(bias), in_hbm(lwt), in_hbm(rwt)
    )
    left_all = lax.all_to_all(left, AXIS, 0, 0, tiled=True)

    code = (residue_chain_index + 8 * residue_real_mask).reshape(1, cols)
    coverage, own_residues, own_sequence, w_mix = cover_all(
        z, sequence_real_mask, sequence_chain_index, code, output_weight
    )

    here = right[None]
    scaled = []
    for step in range(max(len(z.masks) - 1, z.pieces)):
        there = swap_with(here, z.masks[step]) if step < len(z.masks) - 1 else None
        if step < z.pieces:
            gradient, here = lax.optimization_barrier((pair_output_gradient, here))
            scaled.append(scale(z, gradient, own_residues, coverage, step))
        if there is not None:
            there, scaled[-1] = lax.optimization_barrier((there, scaled[-1]))
            here = stack(here, there)
    left_all, here = lax.optimization_barrier((left_all, here))
    keep, give = right_sum(z, left_all, own_residues, w_mix, scaled)
    there = swap_with(here, z.masks[-1])
    of_chip = pair_sum(keep, swap_with(give, 1))
    of_chip, here = lax.optimization_barrier((of_chip, here))
    parts = lax.all_to_all(of_chip, AXIS, 0, 0, tiled=True, axis_index_groups=same_core)

    shares = left_side(z, here, there, coverage, left_all, own_residues, w_mix, scaled)
    shares, parts = lax.optimization_barrier((shares, parts))
    got = lax.all_to_all(shares, AXIS, 0, 0, tiled=True)

    sums, grad = owner(z, parts, got, own_sequence, unit, gain, bias, lwt, rwt)
    alignment_gradient = home(z, grad, unit, inverse, gain)
    there = swap_with(sums, z.masks[0])
    there, alignment_gradient = lax.optimization_barrier((there, alignment_gradient))
    sums = join(z, sums, there)
    for bit in z.masks[1:-1]:
        sums = join(z, sums, swap_with(sums, bit))
    lw_grad, rw_grad, gain_grad, bias_grad, out_grad = finish(z, sums, swap_with(sums, z.masks[-1]))
    return (
        alignment_gradient.reshape(alignment_rows.shape),
        gain_grad.reshape(features),
        bias_grad.reshape(features),
        lw_grad.T,
        rw_grad.T,
        out_grad,
    )


def solution(mesh):
    rows = P(("grp", "dap"), None, None)
    in_specs = (rows, P(), P(), P(), P(), P(), rows, P("grp"), P("grp"), P("grp"), P("grp"))
    out_specs = (rows, P("grp"), P("grp"), P("grp", None), P("grp", None), P("grp", None))
    return jax.shard_map(
        functools.partial(on_device, mesh.shape[AXIS]),
        mesh=mesh,
        in_specs=in_specs,
        out_specs=out_specs,
        check_vma=False,
    )
```

```python
import functools

import jax
import jax.numpy as jnp
from jax import lax
from jax.experimental import pallas as pl
from jax.experimental.pallas import tpu as pltpu
from jax.sharding import PartitionSpec as P

CHAINS = 4
EPSILON = 1e-05
AXIS = "dap"
F32 = jnp.float32
BF16 = jnp.bfloat16
LANES = 128
MIB = 1024 * 1024
VMEM = pl.BlockSpec(memory_space=pltpu.VMEM)


def mm(a, b, dims=(1, 0)):
    return lax.dot_general(
        a, b, (((dims[0],), (dims[1],)), ((), ())), preferred_element_type=F32
    )


def in_hbm(value):
    return pltpu.with_memory_space_constraint(value, pltpu.HBM)


def params(mib):
    return pltpu.CompilerParams(vmem_limit_bytes=mib * MIB)


def cost(microseconds):
    flops = int(microseconds * 1.15e9)
    return pl.CostEstimate(flops=flops, bytes_accessed=0, transcendentals=0)


def sds(shape, dtype):
    return jax.ShapeDtypeStruct(shape, dtype)


def up(n, to=16):
    return -(-n // to) * to


class Sizes:
    def __init__(self, size, res, cols, pair, width, features, seqs):
        self.size, self.res, self.cols, self.pair = size, res, cols, pair
        self.width, self.features, self.seqs = width, features, seqs
        self.chips = size // 2
        self.planes = cols // LANES
        self.wide = width * seqs
        self.groups = max(g for g in (4, 3, 2, 1) if g == 1 or res % (16 * g) == 0)
        self.rows = res // self.groups
        self.slots = up(self.rows)
        self.piece = width * width // size
        self.piece_slots = up(self.piece)
        self.sum_rows = up(2 * width + 2, 8) * features // LANES
        self.block = max(b for b in range(1, 9) if res % b == 0)
        self.blocks = res // self.block
        self.mib = 40 if self.wide <= 1024 else 56
        bits = size.bit_length() - 1
        self.masks = [size >> (b + 1) for b in range(bits)]

    def origin(self, p):
        return sum(m * ((p >> b) & 1) for b, m in enumerate(self.masks))


def normalise(x):
    center = x - jnp.mean(x, axis=-1, keepdims=True)
    inverse = lax.rsqrt(jnp.mean(center * center, axis=-1, keepdims=True) + EPSILON)
    return center * inverse, inverse


def project_kernel(z, x_ref, gain_ref, bias_ref, lwt_ref, rwt_ref,
                   left_ref, right_ref, unit_ref, inverse_ref):
    unit, inverse = normalise(x_ref[...].astype(F32))
    normed = (unit * gain_ref[...] + bias_ref[...]).astype(BF16)
    right_ref[...] = mm(rwt_ref[...], normed, (1, 1)).astype(BF16)
    left = mm(normed, lwt_ref[...], (1, 1))
    for d in range(z.size):
        parts = [
            left[d * z.res + g * z.rows : d * z.res + (g + 1) * z.rows] for g in range(z.groups)
        ]
        parts.append(jnp.zeros((z.rows, LANES - z.groups * z.width), F32))
        packed = jnp.concatenate(parts, axis=1)
        if z.slots > z.rows:
            packed = jnp.concatenate([packed, jnp.zeros((z.slots - z.rows, LANES), F32)], axis=0)
        left_ref[d] = packed.astype(BF16)
    unit_ref[...] = unit
    inverse_ref[...] = inverse


def project(z, x, gain, bias, lwt, rwt):
    return pl.pallas_call(
        functools.partial(project_kernel, z),
        out_shape=(
            sds((z.size, z.slots, LANES), BF16),
            sds((z.width, z.cols), BF16),
            sds((z.cols, z.features), F32),
            sds((z.cols, 1), F32),
        ),
        in_specs=[VMEM] * 5,
        out_specs=(VMEM,) * 4,
        compiler_params=params(16),
        cost_estimate=cost(2.4),
        name="project",
    )(x, gain, bias, lwt, rwt)


def cover_kernel(z, smask_ref, schain_ref, code_ref, w_ref, cover_ref, own_ref, mine_ref, mix_ref,
                 rows):
    me = lax.axis_index(AXIS)
    code = code_ref[...]
    real = (code >= 8).astype(F32)
    chain = code % 8

    def covered(s):
        same = jnp.logical_or(schain_ref[s] == CHAINS, chain == schain_ref[s])
        return jnp.where(same, real * smask_ref[s].astype(F32), 0.0)

    for s in range(z.seqs):
        cover_ref[s : s + 1, :] = covered(s)
    mine_ref[...] = covered(me)
    turned = pltpu.roll(cover_ref[...], z.cols - me * z.res, 1)
    own_ref[...] = jnp.transpose(turned[:, :LANES])[: z.res, :]
    rows[...] = w_ref[...].astype(F32)
    for e in range(z.width):
        part = rows[pl.ds(e, z.width, stride=z.width), :]
        mix_ref[:, e * z.pair : (e + 1) * z.pair] = part.astype(BF16)


def cover_all(z, smask, schain, code, weight):
    smem = pl.BlockSpec(memory_space=pltpu.SMEM)
    return pl.pallas_call(
        functools.partial(cover_kernel, z),
        out_shape=(
            sds((z.seqs, z.cols), F32),
            sds((z.res, z.seqs), F32),
            sds((1, z.cols), F32),
            sds((z.width, z.width * z.pair), BF16),
        ),
        in_specs=[smem, smem, VMEM, VMEM],
        out_specs=(VMEM,) * 4,
        scratch_shapes=[pltpu.VMEM(weight.shape, F32)],
        compiler_params=params(8),
        cost_estimate=cost(1.4),
        name="cover",
    )(smask, schain, code, in_hbm(weight))


def order_left(z, l_ref, own_ref, scratch):
    for s in range(z.seqs):
        got = l_ref[s].astype(F32)
        for g in range(z.groups):
            at = slice(g * z.rows, (g + 1) * z.rows)
            part = got[: z.rows, g * z.width : (g + 1) * z.width] * own_ref[at, s : s + 1]
            scratch[pl.ds(g * z.rows * z.seqs + s, z.rows, stride=z.seqs), :] = part


def block_span(z, step):
    size = z.block * z.pair
    return pl.ds(pl.multiple_of(step * size, size), size)


def right_sum_kernel(z, l_ref, own_ref, cover_ref, w_ref, g_ref, keep_ref, give_ref, scaled_ref,
                     ordered, mixed, total, raw, here, arrived, left_for):
    core = lax.axis_index(AXIS) % 2
    seqs, pair, block = z.seqs, z.pair, z.block

    def fetch(step):
        at = pl.ds(step * block, block)
        return pltpu.make_async_copy(g_ref.at[at], raw.at[at], arrived.at[step])

    def store(step):
        span = slice(step * block * pair, (step + 1) * block * pair)
        return pltpu.make_async_copy(here.at[:, span], scaled_ref.at[:, span], left_for.at[step])

    for step in range(z.blocks):
        fetch(step).start()
    count = mm(cover_ref[...].astype(BF16), own_ref[...].astype(BF16), (0, 1))
    factor = 1.0 / jnp.maximum(count, 1.0)

    def scale(step):
        for i in range(step * block, (step + 1) * block):
            here[:, i * pair : (i + 1) * pair] = (
                raw[i].astype(F32) * factor[:, i : i + 1]
            ).astype(BF16)

    order_left(z, l_ref, own_ref, ordered)
    left = ordered[...].astype(BF16)
    fetch(0).wait()
    scale(0)
    group = 8
    for first in range(0, z.width, group):
        part = mm(left, w_ref[:, first * pair : (first + group) * pair]).astype(BF16)
        for e in range(group):
            for i in range(z.res):
                mixed[(first + e) * seqs : (first + e + 1) * seqs, i * pair : (i + 1) * pair] = part[
                    i * seqs : (i + 1) * seqs, e * pair : (e + 1) * pair
                ]
    store(0).start()

    for step in range(z.blocks):
        if step + 1 < z.blocks:
            fetch(step + 1).wait()
            scale(step + 1)
        span = slice(step * block * pair, (step + 1) * block * pair)
        product = mm(mixed[:, span], here[:, span], (1, 1))
        for c in range(z.planes):
            part = product[:, c * LANES : (c + 1) * LANES]
            total[c] = part if step == 0 else total[c] + part
        if step + 1 < z.blocks:
            store(step + 1).start()

    for chip in range(z.chips):
        for ref, parity in ((keep_ref, core), (give_ref, 1 - core)):
            at = pl.ds(2 * chip + parity, z.width, stride=seqs)
            for c in range(z.planes):
                ref[chip, :, c * LANES : (c + 1) * LANES] = total[c, at, :].astype(BF16)
    for step in range(z.blocks):
        store(step).wait()


def right_sum(z, left, own, cover, weight, gradient):
    out = (z.chips, z.width, z.cols)
    hbm = pl.BlockSpec(memory_space=pltpu.HBM)
    return pl.pallas_call(
        functools.partial(right_sum_kernel, z),
        out_shape=(sds(out, BF16), sds(out, BF16), pltpu.HBM((z.cols, z.res * z.pair), BF16)),
        in_specs=[VMEM] * 4 + [hbm],
        out_specs=(VMEM, VMEM, hbm),
        scratch_shapes=[
            pltpu.VMEM((z.res * z.seqs, z.width), F32),
            pltpu.VMEM((z.wide, z.res * z.pair), BF16),
            pltpu.VMEM((z.planes, z.wide, LANES), F32),
            pltpu.VMEM(gradient.shape, BF16),
            pltpu.VMEM((z.cols, z.res * z.pair), BF16),
            pltpu.SemaphoreType.DMA((z.blocks,)),
            pltpu.SemaphoreType.DMA((z.blocks,)),
        ],
        compiler_params=params(z.mib),
        cost_estimate=cost(13),
        name="right_sum",
    )(left, own, cover, weight, in_hbm(gradient))


def left_side_kernel(z, here_ref, there_ref, cover_ref, l_ref, own_ref, w_ref, s_ref,
                     out_ref, ordered, right, proj, back, wide_rows, here, arrived):
    me = lax.axis_index(AXIS)
    seqs, pair, block, width = z.seqs, z.pair, z.block, z.width

    def fetch(step):
        span = block_span(z, step)
        return pltpu.make_async_copy(s_ref.at[:, span], here.at[:, span], arrived.at[step])

    for step in range(z.blocks):
        fetch(step).start()
    order_left(z, l_ref, own_ref, ordered)
    for side, ref in ((0, here_ref), (z.size // 2, there_ref)):

        @pl.loop(0, z.size // 2)
        def _(p):
            at = pl.ds(me ^ z.origin(p + side), width, stride=seqs)
            for c in range(z.planes):
                wide_rows[c, at, :] = ref[p, :, c * LANES : (c + 1) * LANES].astype(F32)

    for e in range(width):
        at = slice(e * seqs, (e + 1) * seqs)
        for c in range(z.planes):
            lanes = slice(c * LANES, (c + 1) * LANES)
            right[at, lanes] = (wide_rows[c, at, :] * cover_ref[:, lanes]).astype(BF16)

    @pl.loop(0, z.blocks)
    def _(step):
        fetch(step).wait()
        span = block_span(z, step)
        group = width // 4
        for first in range(0, width, group):
            part = mm(right[first * seqs : (first + group) * seqs, :], here[:, span])
            part = part.astype(BF16)
            for i in range(block):
                at = pl.ds(pl.multiple_of((step * block + i) * seqs, seqs), seqs)
                for e in range(group):
                    proj[at, (first + e) * pair : (first + e + 1) * pair] = part[
                        e * seqs : (e + 1) * seqs, i * pair : (i + 1) * pair
                    ]

    back[...] = mm(proj[...], w_ref[...], (1, 1))
    spread = wide_rows.at[0]
    left = ordered[...].astype(BF16)
    for first in range(0, width, 8):
        total = mm(left, proj[:, first * pair : (first + 8) * pair], (0, 0))
        for e in range(8):
            spread[pl.ds(first + e, width, stride=width), :] = total[:, e * pair : (e + 1) * pair]
    for d in range(z.size):
        got = spread[d * z.piece : (d + 1) * z.piece, :]
        if z.piece_slots > z.piece:
            got = jnp.concatenate([got, jnp.zeros((z.piece_slots - z.piece, pair), F32)], axis=0)
        out_ref[d, : z.piece_slots] = got.astype(BF16)
        parts = [
            back[pl.ds(g * z.rows * seqs + d, z.rows, stride=seqs), :] for g in range(z.groups)
        ]
        parts.append(jnp.zeros((z.rows, LANES - z.groups * width), F32))
        packed = jnp.concatenate(parts, axis=1)
        if z.slots > z.rows:
            packed = jnp.concatenate([packed, jnp.zeros((z.slots - z.rows, LANES), F32)], axis=0)
        out_ref[d, z.piece_slots :] = packed.astype(BF16)


def left_side(z, here, there, cover, left, own, weight, scaled):
    return pl.pallas_call(
        functools.partial(left_side_kernel, z),
        out_shape=sds((z.size, z.piece_slots + z.slots, LANES), BF16),
        in_specs=[VMEM] * 6 + [pl.BlockSpec(memory_space=pltpu.HBM)],
        out_specs=VMEM,
        scratch_shapes=[
            pltpu.VMEM((z.res * z.seqs, z.width), F32),
            pltpu.VMEM((z.wide, z.cols), BF16),
            pltpu.VMEM((z.res * z.seqs, z.width * z.pair), BF16),
            pltpu.VMEM((z.res * z.seqs, z.width), F32),
            pltpu.VMEM((z.planes, max(z.wide, z.width * z.width), LANES), F32),
            pltpu.VMEM((z.cols, z.res * z.pair), BF16),
            pltpu.SemaphoreType.DMA((z.blocks,)),
        ],
        compiler_params=params(z.mib),
        cost_estimate=cost(11),
        name="left_side",
    )(here, there, cover, left, own, weight, in_hbm(scaled))


def owner_kernel(z, parts_ref, got_ref, cover_ref, unit_ref, gain_ref, bias_ref, lwt_ref, rwt_ref,
                 sums_ref, grad_ref, rows):
    width = z.width
    cover = cover_ref[...]
    right = parts_ref[0].astype(F32)
    for p in range(1, z.chips):
        right = right + parts_ref[p].astype(F32)
    right = (right * cover).astype(BF16)
    piece = got_ref[0, : z.piece_slots].astype(F32)
    for d in range(1, z.size):
        piece = piece + got_ref[d, : z.piece_slots].astype(F32)
    for d in range(z.size):
        got = got_ref[d, z.piece_slots :].astype(F32)
        for g in range(z.groups):
            first = d * z.res + g * z.rows
            rows[first : first + z.rows, :] = got[: z.rows, g * width : (g + 1) * width]
    column = jnp.transpose(jnp.broadcast_to(cover, (8, z.cols)))[:, :1]
    left = (rows[...] * column).astype(BF16)
    unit = unit_ref[...]
    normed = (unit * gain_ref[...] + bias_ref[...]).astype(BF16)
    grad = mm(left, lwt_ref[...]) + mm(right, rwt_ref[...], (0, 0))
    grad_ref[...] = grad
    pad = up(2 * width + 2, 8) - 2 * width - 2
    sums = jnp.concatenate(
        [
            mm(left, normed, (0, 0)),
            mm(right, normed),
            jnp.sum(grad * unit, axis=0, keepdims=True),
            jnp.sum(grad, axis=0, keepdims=True),
            jnp.zeros((pad, z.features), F32),
        ],
        axis=0,
    )
    half = sums.shape[0]
    for part in range(z.features // LANES):
        sums_ref[part * half : (part + 1) * half, :] = sums[
            :, part * LANES : (part + 1) * LANES
        ].astype(BF16)
    sums_ref[z.sum_rows :, :] = piece.astype(BF16)


def owner(z, parts, got, cover, unit, gain, bias, lwt, rwt):
    return pl.pallas_call(
        functools.partial(owner_kernel, z),
        out_shape=(
            sds((z.sum_rows + z.piece_slots, LANES), BF16),
            sds((z.cols, z.features), F32),
        ),
        in_specs=[VMEM] * 8,
        out_specs=(VMEM, VMEM),
        scratch_shapes=[pltpu.VMEM((z.cols, z.width), F32)],
        compiler_params=params(24),
        cost_estimate=cost(0.9),
        name="owner",
    )(parts, got, cover, unit, gain, bias, lwt, rwt)


def stack_kernel(*refs):
    *parts, out_ref = refs
    size = parts[0].shape[0]
    for p, ref in enumerate(parts):
        out_ref[p * size : (p + 1) * size] = ref[...]


def stack(*parts):
    first = parts[0]
    return pl.pallas_call(
        stack_kernel,
        out_shape=sds((len(parts) * first.shape[0],) + first.shape[1:], first.dtype),
        in_specs=[VMEM] * len(parts),
        out_specs=VMEM,
        compiler_params=params(16),
        cost_estimate=cost(0.4),
        name="stack",
    )(*parts)


def pair_sum_kernel(here_ref, there_ref, out_ref):
    for p in range(here_ref.shape[0]):
        out_ref[p] = (here_ref[p].astype(F32) + there_ref[p].astype(F32)).astype(BF16)


def pair_sum(here, there):
    return pl.pallas_call(
        pair_sum_kernel,
        out_shape=sds(here.shape, BF16),
        in_specs=[VMEM, VMEM],
        out_specs=VMEM,
        compiler_params=params(24),
        cost_estimate=cost(0.8),
        name="pair_sum",
    )(here, there)


def join_kernel(z, here_ref, there_ref, out_ref):
    top, more = z.sum_rows, here_ref.shape[0] - z.sum_rows
    out_ref[:top, :] = (here_ref[:top, :].astype(F32) + there_ref[:top, :].astype(F32)).astype(BF16)
    out_ref[top : top + more, :] = here_ref[top:, :]
    out_ref[top + more :, :] = there_ref[top:, :]


def join(z, here, there):
    rows = 2 * here.shape[0] - z.sum_rows
    return pl.pallas_call(
        functools.partial(join_kernel, z),
        out_shape=sds((rows, LANES), BF16),
        in_specs=[VMEM, VMEM],
        out_specs=VMEM,
        compiler_params=params(8),
        cost_estimate=cost(0.4),
        name="join",
    )(here, there)


def finish_kernel(z, here_ref, there_ref, lw_ref, rw_ref, gain_ref, bias_ref, out_ref):
    me = lax.axis_index(AXIS)
    top, width = z.sum_rows, z.width
    sums = here_ref[:top, :].astype(F32) + there_ref[:top, :].astype(F32)
    half = top // (z.features // LANES)
    for part in range(z.features // LANES):
        at = slice(part * LANES, (part + 1) * LANES)
        lw_ref[:, at] = sums[part * half : part * half + width]
        rw_ref[:, at] = sums[part * half + width : part * half + 2 * width]
        gain_ref[:, at] = sums[part * half + 2 * width : part * half + 2 * width + 1]
        bias_ref[:, at] = sums[part * half + 2 * width + 1 : part * half + 2 * width + 2]
    for p in range(z.size):
        ref = here_ref if p < z.size // 2 else there_ref
        first = top + (p % (z.size // 2)) * z.piece_slots
        at = pl.ds(pl.multiple_of((me ^ z.origin(p)) * z.piece, z.piece), z.piece)
        out_ref[at, :] = ref[first : first + z.piece_slots, :].astype(F32)[: z.piece]


def finish(z, here, there):
    return pl.pallas_call(
        functools.partial(finish_kernel, z),
        out_shape=(
            sds((z.width, z.features), F32),
            sds((z.width, z.features), F32),
            sds((1, z.features), F32),
            sds((1, z.features), F32),
            sds((z.width * z.width, z.pair), F32),
        ),
        in_specs=[VMEM, VMEM],
        out_specs=(VMEM,) * 5,
        compiler_params=params(8),
        cost_estimate=cost(0.9),
        name="finish",
    )(here, there)


def home_kernel(grad_ref, unit_ref, inverse_ref, gain_ref, out_ref):
    unit = unit_ref[...]
    d = grad_ref[...] * gain_ref[...]
    out_ref[...] = (
        inverse_ref[...]
        * (
            d
            - jnp.mean(d, axis=-1, keepdims=True)
            - unit * jnp.mean(d * unit, axis=-1, keepdims=True)
        )
    ).astype(BF16)


def home(z, grad, unit, inverse, gain):
    return pl.pallas_call(
        home_kernel,
        out_shape=sds(unit.shape, BF16),
        in_specs=[VMEM] * 4,
        out_specs=VMEM,
        compiler_params=params(16),
        cost_estimate=cost(1.2),
        name="home",
    )(grad, unit, inverse, gain)


def on_device(
    size,
    alignment_rows,
    norm_gain_vector,
    norm_bias_vector,
    left_weight,
    right_weight,
    output_weight,
    pair_output_gradient,
    sequence_real_mask,
    sequence_chain_index,
    residue_real_mask,
    residue_chain_index,
):
    me = lax.axis_index(AXIS)
    res, cols, pair = pair_output_gradient.shape
    features, width = left_weight.shape
    seqs = sequence_real_mask.shape[0]
    z = Sizes(size, res, cols, pair, width, features, seqs)
    same_core = [[d for d in range(size) if d % 2 == c] for c in (0, 1)]

    def swap_with(value, bit):
        return lax.ppermute(value, AXIS, [(d, d ^ bit) for d in range(size)])

    x = alignment_rows.reshape(cols, features)
    gain = norm_gain_vector.reshape(1, features)
    bias = norm_bias_vector.reshape(1, features)
    lwt, rwt = left_weight.T, right_weight.T
    left, right, unit, inverse = project(
        z, in_hbm(x), in_hbm(gain), in_hbm(bias), in_hbm(lwt), in_hbm(rwt)
    )
    left_all = lax.all_to_all(left, AXIS, 0, 0, tiled=True)

    code = (residue_chain_index + 8 * residue_real_mask).reshape(1, cols)
    coverage, own_residues, own_sequence, w_mix = cover_all(
        z, sequence_real_mask, sequence_chain_index, code, output_weight
    )

    here = right[None]
    for bit in z.masks[:-3]:
        here = stack(here, swap_with(here, bit))
    one, two = z.masks[-3:-1]
    here = stack(here, *[swap_with(here, bit) for bit in (one, two, one ^ two)])
    left_all, here = lax.optimization_barrier((left_all, here))
    there = swap_with(here, z.masks[-1])
    keep, give, scaled = right_sum(
        z, left_all, own_residues, coverage, w_mix, pair_output_gradient
    )
    of_chip = pair_sum(keep, swap_with(give, 1))
    parts = lax.all_to_all(of_chip, AXIS, 0, 0, tiled=True, axis_index_groups=same_core)

    shares = left_side(z, here, there, coverage, left_all, own_residues, w_mix, scaled)
    shares, parts = lax.optimization_barrier((shares, parts))
    got = lax.all_to_all(shares, AXIS, 0, 0, tiled=True)

    sums, grad = owner(z, parts, got, own_sequence, unit, gain, bias, lwt, rwt)
    alignment_gradient = home(z, grad, unit, inverse, gain)
    there = swap_with(sums, z.masks[0])
    there, alignment_gradient = lax.optimization_barrier((there, alignment_gradient))
    sums = join(z, sums, there)
    for bit in z.masks[1:-1]:
        sums = join(z, sums, swap_with(sums, bit))
    lw_grad, rw_grad, gain_grad, bias_grad, out_grad = finish(z, sums, swap_with(sums, z.masks[-1]))
    return (
        alignment_gradient.reshape(alignment_rows.shape),
        gain_grad.reshape(features),
        bias_grad.reshape(features),
        lw_grad.T,
        rw_grad.T,
        out_grad,
    )


def solution(mesh):
    rows = P(("grp", "dap"), None, None)
    in_specs = (rows, P(), P(), P(), P(), P(), rows, P("grp"), P("grp"), P("grp"), P("grp"))
    out_specs = (rows, P("grp"), P("grp"), P("grp", None), P("grp", None), P("grp", None))
    return jax.shard_map(
        functools.partial(on_device, mesh.shape[AXIS]),
        mesh=mesh,
        in_specs=in_specs,
        out_specs=out_specs,
        check_vma=False,
    )
```

```python
import functools

import jax
import jax.numpy as jnp
from jax import lax
from jax.experimental import pallas as pl
from jax.experimental.pallas import tpu as pltpu
from jax.sharding import PartitionSpec as P

CHAINS = 4
EPSILON = 1e-05
AXIS = "dap"
F32 = jnp.float32
BF16 = jnp.bfloat16
LANES = 128
MIB = 1024 * 1024
VMEM = pl.BlockSpec(memory_space=pltpu.VMEM)


def mm(a, b, dims=(1, 0)):
    return lax.dot_general(
        a, b, (((dims[0],), (dims[1],)), ((), ())), preferred_element_type=F32
    )


def in_hbm(value):
    return pltpu.with_memory_space_constraint(value, pltpu.HBM)


def params(mib):
    return pltpu.CompilerParams(vmem_limit_bytes=mib * MIB)


def cost(microseconds):
    flops = int(microseconds * 1.15e9)
    return pl.CostEstimate(flops=flops, bytes_accessed=0, transcendentals=0)


def sds(shape, dtype):
    return jax.ShapeDtypeStruct(shape, dtype)


def up(n, to=16):
    return -(-n // to) * to


class Sizes:
    def __init__(self, size, res, cols, pair, width, features, seqs):
        self.size, self.res, self.cols, self.pair = size, res, cols, pair
        self.width, self.features, self.seqs = width, features, seqs
        self.chips = size // 2
        self.planes = cols // LANES
        self.wide = width * seqs
        self.groups = max(g for g in (4, 3, 2, 1) if g == 1 or res % (16 * g) == 0)
        self.rows = res // self.groups
        self.slots = up(self.rows)
        self.piece = width * width // size
        self.piece_slots = up(self.piece)
        self.sum_rows = up(2 * width + 2, 8) * features // LANES
        self.block = max(b for b in range(1, 9) if res % b == 0)
        self.blocks = res // self.block
        self.mib = 40 if self.wide <= 1024 else 56
        bits = size.bit_length() - 1
        self.masks = [size >> (b + 1) for b in range(bits)]

    def origin(self, p):
        return sum(m * ((p >> b) & 1) for b, m in enumerate(self.masks))


def normalise(x):
    center = x - jnp.mean(x, axis=-1, keepdims=True)
    inverse = lax.rsqrt(jnp.mean(center * center, axis=-1, keepdims=True) + EPSILON)
    return center * inverse, inverse


def project_kernel(z, x_ref, gain_ref, bias_ref, lwt_ref, rwt_ref,
                   left_ref, right_ref, unit_ref, inverse_ref):
    unit, inverse = normalise(x_ref[...].astype(F32))
    normed = (unit * gain_ref[...] + bias_ref[...]).astype(BF16)
    right_ref[...] = mm(rwt_ref[...], normed, (1, 1)).astype(BF16)
    left = mm(normed, lwt_ref[...], (1, 1))
    for d in range(z.size):
        parts = [
            left[d * z.res + g * z.rows : d * z.res + (g + 1) * z.rows] for g in range(z.groups)
        ]
        parts.append(jnp.zeros((z.rows, LANES - z.groups * z.width), F32))
        packed = jnp.concatenate(parts, axis=1)
        if z.slots > z.rows:
            packed = jnp.concatenate([packed, jnp.zeros((z.slots - z.rows, LANES), F32)], axis=0)
        left_ref[d] = packed.astype(BF16)
    unit_ref[...] = unit
    inverse_ref[...] = inverse


def project(z, x, gain, bias, lwt, rwt):
    return pl.pallas_call(
        functools.partial(project_kernel, z),
        out_shape=(
            sds((z.size, z.slots, LANES), BF16),
            sds((z.width, z.cols), BF16),
            sds((z.cols, z.features), F32),
            sds((z.cols, 1), F32),
        ),
        in_specs=[VMEM] * 5,
        out_specs=(VMEM,) * 4,
        compiler_params=params(16),
        cost_estimate=cost(2.4),
        name="project",
    )(x, gain, bias, lwt, rwt)


def cover_kernel(z, smask_ref, schain_ref, code_ref, w_ref, cover_ref, own_ref, mine_ref, mix_ref,
                 rows):
    me = lax.axis_index(AXIS)
    code = code_ref[...]
    real = (code >= 8).astype(F32)
    chain = code % 8

    def covered(s):
        same = jnp.logical_or(schain_ref[s] == CHAINS, chain == schain_ref[s])
        return jnp.where(same, real * smask_ref[s].astype(F32), 0.0)

    for s in range(z.seqs):
        cover_ref[s : s + 1, :] = covered(s)
    mine_ref[...] = covered(me)
    turned = pltpu.roll(cover_ref[...], z.cols - me * z.res, 1)
    own_ref[...] = jnp.transpose(turned[:, :LANES])[: z.res, :]
    rows[...] = w_ref[...].astype(F32)
    for e in range(z.width):
        part = rows[pl.ds(e, z.width, stride=z.width), :]
        mix_ref[:, e * z.pair : (e + 1) * z.pair] = part.astype(BF16)


def cover_all(z, smask, schain, code, weight):
    smem = pl.BlockSpec(memory_space=pltpu.SMEM)
    return pl.pallas_call(
        functools.partial(cover_kernel, z),
        out_shape=(
            sds((z.seqs, z.cols), F32),
            sds((z.res, z.seqs), F32),
            sds((1, z.cols), F32),
            sds((z.width, z.width * z.pair), BF16),
        ),
        in_specs=[smem, smem, VMEM, VMEM],
        out_specs=(VMEM,) * 4,
        scratch_shapes=[pltpu.VMEM(weight.shape, F32)],
        compiler_params=params(8),
        cost_estimate=cost(1.4),
        name="cover",
    )(smask, schain, code, in_hbm(weight))


def order_left(z, l_ref, own_ref, scratch):
    for s in range(z.seqs):
        got = l_ref[s].astype(F32)
        for g in range(z.groups):
            at = slice(g * z.rows, (g + 1) * z.rows)
            part = got[: z.rows, g * z.width : (g + 1) * z.width] * own_ref[at, s : s + 1]
            scratch[pl.ds(g * z.rows * z.seqs + s, z.rows, stride=z.seqs), :] = part


def block_span(z, step):
    size = z.block * z.pair
    return pl.ds(pl.multiple_of(step * size, size), size)


def right_sum_kernel(z, l_ref, own_ref, cover_ref, w_ref, g_ref, keep_ref, give_ref, scaled_ref,
                     ordered, mixed, total, raw, here, arrived, left_for):
    core = lax.axis_index(AXIS) % 2
    seqs, pair, block = z.seqs, z.pair, z.block

    def fetch(step):
        at = pl.ds(step * block, block)
        return pltpu.make_async_copy(g_ref.at[at], raw.at[at], arrived.at[step])

    def store(step):
        span = slice(step * block * pair, (step + 1) * block * pair)
        return pltpu.make_async_copy(here.at[:, span], scaled_ref.at[:, span], left_for.at[step])

    for step in range(z.blocks):
        fetch(step).start()
    count = mm(cover_ref[...].astype(BF16), own_ref[...].astype(BF16), (0, 1))
    factor = 1.0 / jnp.maximum(count, 1.0)

    def scale(step):
        for i in range(step * block, (step + 1) * block):
            here[:, i * pair : (i + 1) * pair] = (
                raw[i].astype(F32) * factor[:, i : i + 1]
            ).astype(BF16)

    order_left(z, l_ref, own_ref, ordered)
    left = ordered[...].astype(BF16)
    group = 8
    for first in range(0, z.width, group):
        part = mm(left, w_ref[:, first * pair : (first + group) * pair]).astype(BF16)
        for e in range(group):
            for i in range(z.res):
                mixed[(first + e) * seqs : (first + e + 1) * seqs, i * pair : (i + 1) * pair] = part[
                    i * seqs : (i + 1) * seqs, e * pair : (e + 1) * pair
                ]
    fetch(0).wait()
    scale(0)
    store(0).start()

    for step in range(z.blocks):
        if step + 1 < z.blocks:
            fetch(step + 1).wait()
            scale(step + 1)
        span = slice(step * block * pair, (step + 1) * block * pair)
        product = mm(mixed[:, span], here[:, span], (1, 1))
        for c in range(z.planes):
            part = product[:, c * LANES : (c + 1) * LANES]
            total[c] = part if step == 0 else total[c] + part
        if step + 1 < z.blocks:
            store(step + 1).start()

    for chip in range(z.chips):
        for ref, parity in ((keep_ref, core), (give_ref, 1 - core)):
            at = pl.ds(2 * chip + parity, z.width, stride=seqs)
            for c in range(z.planes):
                ref[chip, :, c * LANES : (c + 1) * LANES] = total[c, at, :].astype(BF16)
    for step in range(z.blocks):
        store(step).wait()


def right_sum(z, left, own, cover, weight, gradient):
    out = (z.chips, z.width, z.cols)
    hbm = pl.BlockSpec(memory_space=pltpu.HBM)
    return pl.pallas_call(
        functools.partial(right_sum_kernel, z),
        out_shape=(sds(out, BF16), sds(out, BF16), pltpu.HBM((z.cols, z.res * z.pair), BF16)),
        in_specs=[VMEM] * 4 + [hbm],
        out_specs=(VMEM, VMEM, hbm),
        scratch_shapes=[
            pltpu.VMEM((z.res * z.seqs, z.width), F32),
            pltpu.VMEM((z.wide, z.res * z.pair), BF16),
            pltpu.VMEM((z.planes, z.wide, LANES), F32),
            pltpu.VMEM(gradient.shape, BF16),
            pltpu.VMEM((z.cols, z.res * z.pair), BF16),
            pltpu.SemaphoreType.DMA((z.blocks,)),
            pltpu.SemaphoreType.DMA((z.blocks,)),
        ],
        compiler_params=params(z.mib),
        cost_estimate=cost(13),
        name="right_sum",
    )(left, own, cover, weight, in_hbm(gradient))


def left_side_kernel(z, here_ref, there_ref, cover_ref, l_ref, own_ref, w_ref, s_ref,
                     out_ref, ordered, right, proj, back, wide_rows, here, arrived):
    me = lax.axis_index(AXIS)
    seqs, pair, block, width = z.seqs, z.pair, z.block, z.width

    def fetch(step):
        span = block_span(z, step)
        return pltpu.make_async_copy(s_ref.at[:, span], here.at[:, span], arrived.at[step])

    for step in range(z.blocks):
        fetch(step).start()
    order_left(z, l_ref, own_ref, ordered)
    for side, ref in ((0, here_ref), (z.size // 2, there_ref)):

        @pl.loop(0, z.size // 2)
        def _(p):
            at = pl.ds(me ^ z.origin(p + side), width, stride=seqs)
            for c in range(z.planes):
                wide_rows[c, at, :] = ref[p, :, c * LANES : (c + 1) * LANES].astype(F32)

    for e in range(width):
        at = slice(e * seqs, (e + 1) * seqs)
        for c in range(z.planes):
            lanes = slice(c * LANES, (c + 1) * LANES)
            right[at, lanes] = (wide_rows[c, at, :] * cover_ref[:, lanes]).astype(BF16)

    @pl.loop(0, z.blocks)
    def _(step):
        fetch(step).wait()
        span = block_span(z, step)
        group = width // 4
        for first in range(0, width, group):
            part = mm(right[first * seqs : (first + group) * seqs, :], here[:, span])
            part = part.astype(BF16)
            for i in range(block):
                at = pl.ds(pl.multiple_of((step * block + i) * seqs, seqs), seqs)
                for e in range(group):
                    proj[at, (first + e) * pair : (first + e + 1) * pair] = part[
                        e * seqs : (e + 1) * seqs, i * pair : (i + 1) * pair
                    ]

    back[...] = mm(proj[...], w_ref[...], (1, 1))
    spread = wide_rows.at[0]
    left = ordered[...].astype(BF16)
    for first in range(0, width, 8):
        total = mm(left, proj[:, first * pair : (first + 8) * pair], (0, 0))
        for e in range(8):
            spread[pl.ds(first + e, width, stride=width), :] = total[:, e * pair : (e + 1) * pair]
    for d in range(z.size):
        got = spread[d * z.piece : (d + 1) * z.piece, :]
        if z.piece_slots > z.piece:
            got = jnp.concatenate([got, jnp.zeros((z.piece_slots - z.piece, pair), F32)], axis=0)
        out_ref[d, : z.piece_slots] = got.astype(BF16)
        parts = [
            back[pl.ds(g * z.rows * seqs + d, z.rows, stride=seqs), :] for g in range(z.groups)
        ]
        parts.append(jnp.zeros((z.rows, LANES - z.groups * width), F32))
        packed = jnp.concatenate(parts, axis=1)
        if z.slots > z.rows:
            packed = jnp.concatenate([packed, jnp.zeros((z.slots - z.rows, LANES), F32)], axis=0)
        out_ref[d, z.piece_slots :] = packed.astype(BF16)


def left_side(z, here, there, cover, left, own, weight, scaled):
    return pl.pallas_call(
        functools.partial(left_side_kernel, z),
        out_shape=sds((z.size, z.piece_slots + z.slots, LANES), BF16),
        in_specs=[VMEM] * 6 + [pl.BlockSpec(memory_space=pltpu.HBM)],
        out_specs=VMEM,
        scratch_shapes=[
            pltpu.VMEM((z.res * z.seqs, z.width), F32),
            pltpu.VMEM((z.wide, z.cols), BF16),
            pltpu.VMEM((z.res * z.seqs, z.width * z.pair), BF16),
            pltpu.VMEM((z.res * z.seqs, z.width), F32),
            pltpu.VMEM((z.planes, max(z.wide, z.width * z.width), LANES), F32),
            pltpu.VMEM((z.cols, z.res * z.pair), BF16),
            pltpu.SemaphoreType.DMA((z.blocks,)),
        ],
        compiler_params=params(z.mib),
        cost_estimate=cost(11),
        name="left_side",
    )(here, there, cover, left, own, weight, in_hbm(scaled))


def owner_kernel(z, parts_ref, got_ref, cover_ref, unit_ref, gain_ref, bias_ref, lwt_ref, rwt_ref,
                 sums_ref, grad_ref, rows):
    width = z.width
    cover = cover_ref[...]
    right = parts_ref[0].astype(F32)
    for p in range(1, z.chips):
        right = right + parts_ref[p].astype(F32)
    right = (right * cover).astype(BF16)
    piece = got_ref[0, : z.piece_slots].astype(F32)
    for d in range(1, z.size):
        piece = piece + got_ref[d, : z.piece_slots].astype(F32)
    for d in range(z.size):
        got = got_ref[d, z.piece_slots :].astype(F32)
        for g in range(z.groups):
            first = d * z.res + g * z.rows
            rows[first : first + z.rows, :] = got[: z.rows, g * width : (g + 1) * width]
    column = jnp.transpose(jnp.broadcast_to(cover, (8, z.cols)))[:, :1]
    left = (rows[...] * column).astype(BF16)
    unit = unit_ref[...]
    normed = (unit * gain_ref[...] + bias_ref[...]).astype(BF16)
    grad = mm(left, lwt_ref[...]) + mm(right, rwt_ref[...], (0, 0))
    grad_ref[...] = grad
    pad = up(2 * width + 2, 8) - 2 * width - 2
    sums = jnp.concatenate(
        [
            mm(left, normed, (0, 0)),
            mm(right, normed),
            jnp.sum(grad * unit, axis=0, keepdims=True),
            jnp.sum(grad, axis=0, keepdims=True),
            jnp.zeros((pad, z.features), F32),
        ],
        axis=0,
    )
    half = sums.shape[0]
    for part in range(z.features // LANES):
        sums_ref[part * half : (part + 1) * half, :] = sums[
            :, part * LANES : (part + 1) * LANES
        ].astype(BF16)
    sums_ref[z.sum_rows :, :] = piece.astype(BF16)


def owner(z, parts, got, cover, unit, gain, bias, lwt, rwt):
    return pl.pallas_call(
        functools.partial(owner_kernel, z),
        out_shape=(
            sds((z.sum_rows + z.piece_slots, LANES), BF16),
            sds((z.cols, z.features), F32),
        ),
        in_specs=[VMEM] * 8,
        out_specs=(VMEM, VMEM),
        scratch_shapes=[pltpu.VMEM((z.cols, z.width), F32)],
        compiler_params=params(24),
        cost_estimate=cost(0.9),
        name="owner",
    )(parts, got, cover, unit, gain, bias, lwt, rwt)


def stack_kernel(*refs):
    *parts, out_ref = refs
    size = parts[0].shape[0]
    for p, ref in enumerate(parts):
        out_ref[p * size : (p + 1) * size] = ref[...]


def stack(*parts):
    first = parts[0]
    return pl.pallas_call(
        stack_kernel,
        out_shape=sds((len(parts) * first.shape[0],) + first.shape[1:], first.dtype),
        in_specs=[VMEM] * len(parts),
        out_specs=VMEM,
        compiler_params=params(16),
        cost_estimate=cost(0.4),
        name="stack",
    )(*parts)


def pair_sum_kernel(here_ref, there_ref, out_ref):
    for p in range(here_ref.shape[0]):
        out_ref[p] = (here_ref[p].astype(F32) + there_ref[p].astype(F32)).astype(BF16)


def pair_sum(here, there):
    return pl.pallas_call(
        pair_sum_kernel,
        out_shape=sds(here.shape, BF16),
        in_specs=[VMEM, VMEM],
        out_specs=VMEM,
        compiler_params=params(24),
        cost_estimate=cost(0.8),
        name="pair_sum",
    )(here, there)


def join_kernel(z, *refs):
    *parts, out_ref = refs
    top, more = z.sum_rows, parts[0].shape[0] - z.sum_rows
    sums = [ref[:top, :].astype(F32) for ref in parts]
    while len(sums) > 1:
        sums = [one + two for one, two in zip(sums[::2], sums[1::2])]
    out_ref[:top, :] = sums[0].astype(BF16)
    for p, ref in enumerate(parts):
        out_ref[top + p * more : top + (p + 1) * more, :] = ref[top:, :]


def join(z, *parts):
    rows = z.sum_rows + len(parts) * (parts[0].shape[0] - z.sum_rows)
    return pl.pallas_call(
        functools.partial(join_kernel, z),
        out_shape=sds((rows, LANES), BF16),
        in_specs=[VMEM] * len(parts),
        out_specs=VMEM,
        compiler_params=params(8),
        cost_estimate=cost(0.4),
        name="join",
    )(*parts)


def finish_kernel(z, here_ref, there_ref, lw_ref, rw_ref, gain_ref, bias_ref, out_ref):
    me = lax.axis_index(AXIS)
    top, width = z.sum_rows, z.width
    sums = here_ref[:top, :].astype(F32) + there_ref[:top, :].astype(F32)
    half = top // (z.features // LANES)
    for part in range(z.features // LANES):
        at = slice(part * LANES, (part + 1) * LANES)
        lw_ref[:, at] = sums[part * half : part * half + width]
        rw_ref[:, at] = sums[part * half + width : part * half + 2 * width]
        gain_ref[:, at] = sums[part * half + 2 * width : part * half + 2 * width + 1]
        bias_ref[:, at] = sums[part * half + 2 * width + 1 : part * half + 2 * width + 2]
    for p in range(z.size):
        ref = here_ref if p < z.size // 2 else there_ref
        first = top + (p % (z.size // 2)) * z.piece_slots
        at = pl.ds(pl.multiple_of((me ^ z.origin(p)) * z.piece, z.piece), z.piece)
        out_ref[at, :] = ref[first : first + z.piece_slots, :].astype(F32)[: z.piece]


def finish(z, here, there):
    return pl.pallas_call(
        functools.partial(finish_kernel, z),
        out_shape=(
            sds((z.width, z.features), F32),
            sds((z.width, z.features), F32),
            sds((1, z.features), F32),
            sds((1, z.features), F32),
            sds((z.width * z.width, z.pair), F32),
        ),
        in_specs=[VMEM, VMEM],
        out_specs=(VMEM,) * 5,
        compiler_params=params(8),
        cost_estimate=cost(0.9),
        name="finish",
    )(here, there)


def home_kernel(grad_ref, unit_ref, inverse_ref, gain_ref, out_ref):
    unit = unit_ref[...]
    d = grad_ref[...] * gain_ref[...]
    out_ref[...] = (
        inverse_ref[...]
        * (
            d
            - jnp.mean(d, axis=-1, keepdims=True)
            - unit * jnp.mean(d * unit, axis=-1, keepdims=True)
        )
    ).astype(BF16)


def home(z, grad, unit, inverse, gain):
    return pl.pallas_call(
        home_kernel,
        out_shape=sds(unit.shape, BF16),
        in_specs=[VMEM] * 4,
        out_specs=VMEM,
        compiler_params=params(16),
        cost_estimate=cost(1.2),
        name="home",
    )(grad, unit, inverse, gain)


def on_device(
    size,
    alignment_rows,
    norm_gain_vector,
    norm_bias_vector,
    left_weight,
    right_weight,
    output_weight,
    pair_output_gradient,
    sequence_real_mask,
    sequence_chain_index,
    residue_real_mask,
    residue_chain_index,
):
    me = lax.axis_index(AXIS)
    res, cols, pair = pair_output_gradient.shape
    features, width = left_weight.shape
    seqs = sequence_real_mask.shape[0]
    z = Sizes(size, res, cols, pair, width, features, seqs)
    same_core = [[d for d in range(size) if d % 2 == c] for c in (0, 1)]

    def swap_with(value, bit):
        return lax.ppermute(value, AXIS, [(d, d ^ bit) for d in range(size)])

    x = alignment_rows.reshape(cols, features)
    gain = norm_gain_vector.reshape(1, features)
    bias = norm_bias_vector.reshape(1, features)
    lwt, rwt = left_weight.T, right_weight.T
    left, right, unit, inverse = project(
        z, in_hbm(x), in_hbm(gain), in_hbm(bias), in_hbm(lwt), in_hbm(rwt)
    )
    left_all = lax.all_to_all(left, AXIS, 0, 0, tiled=True)

    code = (residue_chain_index + 8 * residue_real_mask).reshape(1, cols)
    coverage, own_residues, own_sequence, w_mix = cover_all(
        z, sequence_real_mask, sequence_chain_index, code, output_weight
    )

    here = right[None]
    for bit in z.masks[:-3]:
        here = stack(here, swap_with(here, bit))
    one, two = z.masks[-3:-1]
    here = stack(here, *[swap_with(here, bit) for bit in (one, two, one ^ two)])
    left_all, here = lax.optimization_barrier((left_all, here))
    there = swap_with(here, z.masks[-1])
    keep, give, scaled = right_sum(
        z, left_all, own_residues, coverage, w_mix, pair_output_gradient
    )
    of_chip = pair_sum(keep, swap_with(give, 1))
    parts = lax.all_to_all(of_chip, AXIS, 0, 0, tiled=True, axis_index_groups=same_core)

    shares = left_side(z, here, there, coverage, left_all, own_residues, w_mix, scaled)
    shares, parts = lax.optimization_barrier((shares, parts))
    got = lax.all_to_all(shares, AXIS, 0, 0, tiled=True)

    sums, grad = owner(z, parts, got, own_sequence, unit, gain, bias, lwt, rwt)
    alignment_gradient = home(z, grad, unit, inverse, gain)
    for step, bit in enumerate(z.masks[:-3]):
        there = swap_with(sums, bit)
        if step == 0:
            there, alignment_gradient = lax.optimization_barrier((there, alignment_gradient))
        sums = join(z, sums, there)
    sums = join(z, sums, *[swap_with(sums, bit) for bit in (one, two, one ^ two)])
    lw_grad, rw_grad, gain_grad, bias_grad, out_grad = finish(z, sums, swap_with(sums, z.masks[-1]))
    return (
        alignment_gradient.reshape(alignment_rows.shape),
        gain_grad.reshape(features),
        bias_grad.reshape(features),
        lw_grad.T,
        rw_grad.T,
        out_grad,
    )


def solution(mesh):
    rows = P(("grp", "dap"), None, None)
    in_specs = (rows, P(), P(), P(), P(), P(), rows, P("grp"), P("grp"), P("grp"), P("grp"))
    out_specs = (rows, P("grp"), P("grp"), P("grp", None), P("grp", None), P("grp", None))
    return jax.shard_map(
        functools.partial(on_device, mesh.shape[AXIS]),
        mesh=mesh,
        in_specs=in_specs,
        out_specs=out_specs,
        check_vma=False,
    )
```

```python
import functools

import jax
import jax.numpy as jnp
from jax import lax
from jax.experimental import pallas as pl
from jax.experimental.pallas import tpu as pltpu
from jax.sharding import PartitionSpec as P

CHAINS = 4
EPSILON = 1e-05
AXIS = "dap"
F32 = jnp.float32
BF16 = jnp.bfloat16
LANES = 128
MIB = 1024 * 1024
VMEM = pl.BlockSpec(memory_space=pltpu.VMEM)


def mm(a, b, dims=(1, 0)):
    return lax.dot_general(
        a, b, (((dims[0],), (dims[1],)), ((), ())), preferred_element_type=F32
    )


def in_hbm(value):
    return pltpu.with_memory_space_constraint(value, pltpu.HBM)


def params(mib):
    return pltpu.CompilerParams(vmem_limit_bytes=mib * MIB)


def in_vmem(value):
    return pltpu.with_memory_space_constraint(value, pltpu.VMEM)


def cost(microseconds):
    flops = int(microseconds * 1.15e9)
    return pl.CostEstimate(flops=flops, bytes_accessed=0, transcendentals=0)


def sds(shape, dtype):
    return jax.ShapeDtypeStruct(shape, dtype)


def up(n, to=16):
    return -(-n // to) * to


class Sizes:
    def __init__(self, size, res, cols, pair, width, features, seqs):
        self.size, self.res, self.cols, self.pair = size, res, cols, pair
        self.width, self.features, self.seqs = width, features, seqs
        self.chips = size // 2
        self.planes = cols // LANES
        self.wide = width * seqs
        self.groups = max(g for g in (4, 3, 2, 1) if g == 1 or res % (16 * g) == 0)
        self.rows = res // self.groups
        self.slots = up(self.rows)
        self.piece = width * width // size
        self.piece_slots = up(self.piece)
        self.sum_rows = up(2 * width + 2, 8) * features // LANES
        self.block = max(b for b in range(1, 9) if res % b == 0)
        self.blocks = res // self.block
        self.mib = 40 if self.wide <= 1024 else 56
        bits = size.bit_length() - 1
        self.masks = [size >> (b + 1) for b in range(bits)]

    def origin(self, p):
        return sum(m * ((p >> b) & 1) for b, m in enumerate(self.masks))


def normalise(x):
    center = x - jnp.mean(x, axis=-1, keepdims=True)
    inverse = lax.rsqrt(jnp.mean(center * center, axis=-1, keepdims=True) + EPSILON)
    return center * inverse, inverse


def project_kernel(z, x_ref, gain_ref, bias_ref, lwt_ref, rwt_ref,
                   left_ref, right_ref, unit_ref, inverse_ref):
    unit, inverse = normalise(x_ref[...].astype(F32))
    normed = (unit * gain_ref[...] + bias_ref[...]).astype(BF16)
    right_ref[...] = mm(rwt_ref[...], normed, (1, 1)).astype(BF16)
    left = mm(normed, lwt_ref[...], (1, 1))
    for d in range(z.size):
        parts = [
            left[d * z.res + g * z.rows : d * z.res + (g + 1) * z.rows] for g in range(z.groups)
        ]
        parts.append(jnp.zeros((z.rows, LANES - z.groups * z.width), F32))
        packed = jnp.concatenate(parts, axis=1)
        if z.slots > z.rows:
            packed = jnp.concatenate([packed, jnp.zeros((z.slots - z.rows, LANES), F32)], axis=0)
        left_ref[d] = packed.astype(BF16)
    unit_ref[...] = unit
    inverse_ref[...] = inverse


def project(z, x, gain, bias, lwt, rwt):
    return pl.pallas_call(
        functools.partial(project_kernel, z),
        out_shape=(
            sds((z.size, z.slots, LANES), BF16),
            sds((z.width, z.cols), BF16),
            sds((z.cols, z.features), F32),
            sds((z.cols, 1), F32),
        ),
        in_specs=[VMEM] * 5,
        out_specs=(VMEM,) * 4,
        compiler_params=params(16),
        cost_estimate=cost(2.4),
        name="project",
    )(x, gain, bias, lwt, rwt)


def cover_kernel(z, smask_ref, schain_ref, code_ref, w_ref, cover_ref, own_ref, mine_ref, mix_ref,
                 rows):
    me = lax.axis_index(AXIS)
    code = code_ref[...]
    real = (code >= 8).astype(F32)
    chain = code % 8

    def covered(s):
        same = jnp.logical_or(schain_ref[s] == CHAINS, chain == schain_ref[s])
        return jnp.where(same, real * smask_ref[s].astype(F32), 0.0)

    for s in range(z.seqs):
        cover_ref[s : s + 1, :] = covered(s)
    mine_ref[...] = covered(me)
    turned = pltpu.roll(cover_ref[...], z.cols - me * z.res, 1)
    own_ref[...] = jnp.transpose(turned[:, :LANES])[: z.res, :]
    rows[...] = w_ref[...].astype(F32)
    for e in range(z.width):
        part = rows[pl.ds(e, z.width, stride=z.width), :]
        mix_ref[:, e * z.pair : (e + 1) * z.pair] = part.astype(BF16)


def cover_all(z, smask, schain, code, weight):
    smem = pl.BlockSpec(memory_space=pltpu.SMEM)
    return pl.pallas_call(
        functools.partial(cover_kernel, z),
        out_shape=(
            sds((z.seqs, z.cols), F32),
            sds((z.res, z.seqs), F32),
            sds((1, z.cols), F32),
            sds((z.width, z.width * z.pair), BF16),
        ),
        in_specs=[smem, smem, VMEM, VMEM],
        out_specs=(VMEM,) * 4,
        scratch_shapes=[pltpu.VMEM(weight.shape, F32)],
        compiler_params=params(8),
        cost_estimate=cost(1.4),
        name="cover",
    )(smask, schain, code, in_hbm(weight))


def order_left(z, l_ref, own_ref, scratch):
    for s in range(z.seqs):
        got = l_ref[s].astype(F32)
        for g in range(z.groups):
            at = slice(g * z.rows, (g + 1) * z.rows)
            part = got[: z.rows, g * z.width : (g + 1) * z.width] * own_ref[at, s : s + 1]
            scratch[pl.ds(g * z.rows * z.seqs + s, z.rows, stride=z.seqs), :] = part


def block_span(z, step):
    size = z.block * z.pair
    return pl.ds(pl.multiple_of(step * size, size), size)


def mix_kernel(z, l_ref, own_ref, w_ref, mixed, ordered):
    seqs, pair = z.seqs, z.pair
    order_left(z, l_ref, own_ref, ordered)
    left = ordered[...].astype(BF16)
    group = 8
    for first in range(0, z.width, group):
        part = mm(left, w_ref[:, first * pair : (first + group) * pair]).astype(BF16)
        for e in range(group):
            for i in range(z.res):
                mixed[(first + e) * seqs : (first + e + 1) * seqs, i * pair : (i + 1) * pair] = part[
                    i * seqs : (i + 1) * seqs, e * pair : (e + 1) * pair
                ]


def mix(z, left, own, weight):
    return pl.pallas_call(
        functools.partial(mix_kernel, z),
        out_shape=pltpu.VMEM((z.wide, z.res * z.pair), BF16),
        in_specs=[VMEM] * 3,
        out_specs=VMEM,
        scratch_shapes=[pltpu.VMEM((z.res * z.seqs, z.width), F32)],
        compiler_params=params(z.mib // 2),
        cost_estimate=cost(2),
        name="mix",
    )(left, own, weight)


def right_sum_kernel(z, mixed, own_ref, cover_ref, g_ref, keep_ref, give_ref, scaled_ref, total,
                     raw, here, arrived, left_for):
    core = lax.axis_index(AXIS) % 2
    seqs, pair, block = z.seqs, z.pair, z.block

    def fetch(step):
        at = pl.ds(step * block, block)
        return pltpu.make_async_copy(g_ref.at[at], raw.at[at], arrived.at[step])

    def store(step):
        span = slice(step * block * pair, (step + 1) * block * pair)
        return pltpu.make_async_copy(here.at[:, span], scaled_ref.at[:, span], left_for.at[step])

    for step in range(z.blocks):
        fetch(step).start()
    count = mm(cover_ref[...].astype(BF16), own_ref[...].astype(BF16), (0, 1))
    factor = 1.0 / jnp.maximum(count, 1.0)

    def scale(step):
        for i in range(step * block, (step + 1) * block):
            here[:, i * pair : (i + 1) * pair] = (
                raw[i].astype(F32) * factor[:, i : i + 1]
            ).astype(BF16)

    fetch(0).wait()
    scale(0)
    store(0).start()

    for step in range(z.blocks):
        if step + 1 < z.blocks:
            fetch(step + 1).wait()
            scale(step + 1)
        span = slice(step * block * pair, (step + 1) * block * pair)
        product = mm(mixed[:, span], here[:, span], (1, 1))
        for c in range(z.planes):
            part = product[:, c * LANES : (c + 1) * LANES]
            total[c] = part if step == 0 else total[c] + part
        if step + 1 < z.blocks:
            store(step + 1).start()

    for chip in range(z.chips):
        for ref, parity in ((keep_ref, core), (give_ref, 1 - core)):
            at = pl.ds(2 * chip + parity, z.width, stride=seqs)
            for c in range(z.planes):
                ref[chip, :, c * LANES : (c + 1) * LANES] = total[c, at, :].astype(BF16)
    for step in range(z.blocks):
        store(step).wait()


def right_sum(z, mixed, own, cover, gradient):
    out = (z.chips, z.width, z.cols)
    hbm = pl.BlockSpec(memory_space=pltpu.HBM)
    return pl.pallas_call(
        functools.partial(right_sum_kernel, z),
        out_shape=(sds(out, BF16), sds(out, BF16), pltpu.HBM((z.cols, z.res * z.pair), BF16)),
        in_specs=[VMEM] * 3 + [hbm],
        out_specs=(VMEM, VMEM, hbm),
        scratch_shapes=[
            pltpu.VMEM((z.planes, z.wide, LANES), F32),
            pltpu.VMEM(gradient.shape, BF16),
            pltpu.VMEM((z.cols, z.res * z.pair), BF16),
            pltpu.SemaphoreType.DMA((z.blocks,)),
            pltpu.SemaphoreType.DMA((z.blocks,)),
        ],
        compiler_params=params(z.mib),
        cost_estimate=cost(13),
        name="right_sum",
    )(in_vmem(mixed), own, cover, in_hbm(gradient))


def left_side_kernel(z, here_ref, there_ref, cover_ref, l_ref, own_ref, w_ref, s_ref,
                     keep_ref, give_ref, ordered, right, proj, back, wide_rows, here, arrived):
    me = lax.axis_index(AXIS)
    seqs, pair, block, width = z.seqs, z.pair, z.block, z.width

    def fetch(step):
        span = block_span(z, step)
        return pltpu.make_async_copy(s_ref.at[:, span], here.at[:, span], arrived.at[step])

    for step in range(z.blocks):
        fetch(step).start()
    order_left(z, l_ref, own_ref, ordered)
    for side, ref in ((0, here_ref), (z.size // 2, there_ref)):

        @pl.loop(0, z.size // 2)
        def _(p):
            at = pl.ds(me ^ z.origin(p + side), width, stride=seqs)
            for c in range(z.planes):
                wide_rows[c, at, :] = ref[p, :, c * LANES : (c + 1) * LANES].astype(F32)

    for e in range(width):
        at = slice(e * seqs, (e + 1) * seqs)
        for c in range(z.planes):
            lanes = slice(c * LANES, (c + 1) * LANES)
            right[at, lanes] = (wide_rows[c, at, :] * cover_ref[:, lanes]).astype(BF16)

    @pl.loop(0, z.blocks)
    def _(step):
        fetch(step).wait()
        span = block_span(z, step)
        group = width // 4
        for first in range(0, width, group):
            part = mm(right[first * seqs : (first + group) * seqs, :], here[:, span])
            part = part.astype(BF16)
            for i in range(block):
                at = pl.ds(pl.multiple_of((step * block + i) * seqs, seqs), seqs)
                for e in range(group):
                    proj[at, (first + e) * pair : (first + e + 1) * pair] = part[
                        e * seqs : (e + 1) * seqs, i * pair : (i + 1) * pair
                    ]

    back[...] = mm(proj[...], w_ref[...], (1, 1))
    spread = wide_rows.at[0]
    left = ordered[...].astype(BF16)
    for first in range(0, width, 8):
        total = mm(left, proj[:, first * pair : (first + 8) * pair], (0, 0))
        for e in range(8):
            spread[pl.ds(first + e, width, stride=width), :] = total[:, e * pair : (e + 1) * pair]
    for chip in range(z.chips):
        for ref, parity in ((keep_ref, me % 2), (give_ref, 1 - me % 2)):
            d = 2 * chip + parity
            got = spread[pl.ds(pl.multiple_of(d * z.piece, z.piece), z.piece), :]
            if z.piece_slots > z.piece:
                got = jnp.concatenate(
                    [got, jnp.zeros((z.piece_slots - z.piece, pair), F32)], axis=0
                )
            ref[chip, : z.piece_slots] = got.astype(BF16)
            parts = [
                back[pl.ds(g * z.rows * seqs + d, z.rows, stride=seqs), :]
                for g in range(z.groups)
            ]
            parts.append(jnp.zeros((z.rows, LANES - z.groups * width), F32))
            packed = jnp.concatenate(parts, axis=1)
            if z.slots > z.rows:
                packed = jnp.concatenate(
                    [packed, jnp.zeros((z.slots - z.rows, LANES), F32)], axis=0
                )
            ref[chip, z.piece_slots :] = packed.astype(BF16)


def left_side(z, here, there, cover, left, own, weight, scaled):
    return pl.pallas_call(
        functools.partial(left_side_kernel, z),
        out_shape=(sds((z.chips, z.piece_slots + z.slots, LANES), BF16),) * 2,
        in_specs=[VMEM] * 6 + [pl.BlockSpec(memory_space=pltpu.HBM)],
        out_specs=(VMEM, VMEM),
        scratch_shapes=[
            pltpu.VMEM((z.res * z.seqs, z.width), F32),
            pltpu.VMEM((z.wide, z.cols), BF16),
            pltpu.VMEM((z.res * z.seqs, z.width * z.pair), BF16),
            pltpu.VMEM((z.res * z.seqs, z.width), F32),
            pltpu.VMEM((z.planes, max(z.wide, z.width * z.width), LANES), F32),
            pltpu.VMEM((z.cols, z.res * z.pair), BF16),
            pltpu.SemaphoreType.DMA((z.blocks,)),
        ],
        compiler_params=params(z.mib),
        cost_estimate=cost(11),
        name="left_side",
    )(here, there, cover, left, own, weight, in_hbm(scaled))


def owner_kernel(z, parts_ref, got_ref, cover_ref, unit_ref, gain_ref, bias_ref, lwt_ref, rwt_ref,
                 sums_ref, grad_ref, rows):
    width = z.width
    cover = cover_ref[...]
    right = parts_ref[0].astype(F32)
    for p in range(1, z.chips):
        right = right + parts_ref[p].astype(F32)
    right = (right * cover).astype(BF16)
    piece = got_ref[0, : z.piece_slots].astype(F32)
    for chip in range(1, z.chips):
        piece = piece + got_ref[chip, : z.piece_slots].astype(F32)
    core = lax.axis_index(AXIS) % 2
    for parity in (0, 1):

        @pl.when(core == parity)
        def _():
            for chip in range(z.chips):
                for other in (0, 1):
                    at = z.piece_slots + other * z.slots
                    got = got_ref[chip, at : at + z.slots].astype(F32)
                    for g in range(z.groups):
                        first = (2 * chip + (parity ^ other)) * z.res + g * z.rows
                        rows[first : first + z.rows, :] = got[
                            : z.rows, g * width : (g + 1) * width
                        ]

    column = jnp.transpose(jnp.broadcast_to(cover, (8, z.cols)))[:, :1]
    left = (rows[...] * column).astype(BF16)
    unit = unit_ref[...]
    normed = (unit * gain_ref[...] + bias_ref[...]).astype(BF16)
    grad = mm(left, lwt_ref[...]) + mm(right, rwt_ref[...], (0, 0))
    grad_ref[...] = grad
    pad = up(2 * width + 2, 8) - 2 * width - 2
    sums = jnp.concatenate(
        [
            mm(left, normed, (0, 0)),
            mm(right, normed),
            jnp.sum(grad * unit, axis=0, keepdims=True),
            jnp.sum(grad, axis=0, keepdims=True),
            jnp.zeros((pad, z.features), F32),
        ],
        axis=0,
    )
    half = sums.shape[0]
    for part in range(z.features // LANES):
        sums_ref[part * half : (part + 1) * half, :] = sums[
            :, part * LANES : (part + 1) * LANES
        ].astype(BF16)
    sums_ref[z.sum_rows :, :] = piece.astype(BF16)


def owner(z, parts, got, cover, unit, gain, bias, lwt, rwt):
    return pl.pallas_call(
        functools.partial(owner_kernel, z),
        out_shape=(
            sds((z.sum_rows + z.piece_slots, LANES), BF16),
            sds((z.cols, z.features), F32),
        ),
        in_specs=[VMEM] * 8,
        out_specs=(VMEM, VMEM),
        scratch_shapes=[pltpu.VMEM((z.cols, z.width), F32)],
        compiler_params=params(24),
        cost_estimate=cost(0.9),
        name="owner",
    )(parts, got, cover, unit, gain, bias, lwt, rwt)


def stack_kernel(*refs):
    *parts, out_ref = refs
    size = parts[0].shape[0]
    for p, ref in enumerate(parts):
        out_ref[p * size : (p + 1) * size] = ref[...]


def stack(*parts):
    first = parts[0]
    return pl.pallas_call(
        stack_kernel,
        out_shape=sds((len(parts) * first.shape[0],) + first.shape[1:], first.dtype),
        in_specs=[VMEM] * len(parts),
        out_specs=VMEM,
        compiler_params=params(16),
        cost_estimate=cost(0.4),
        name="stack",
    )(*parts)


def pair_sum_kernel(here_ref, there_ref, out_ref):
    for p in range(here_ref.shape[0]):
        out_ref[p] = (here_ref[p].astype(F32) + there_ref[p].astype(F32)).astype(BF16)


def pair_sum(here, there):
    return pl.pallas_call(
        pair_sum_kernel,
        out_shape=sds(here.shape, BF16),
        in_specs=[VMEM, VMEM],
        out_specs=VMEM,
        compiler_params=params(24),
        cost_estimate=cost(0.8),
        name="pair_sum",
    )(here, there)


def chip_share_kernel(z, here_ref, there_ref, out_ref):
    top, both = z.piece_slots, z.piece_slots + z.slots
    for chip in range(z.chips):
        out_ref[chip, :top] = (
            here_ref[chip, :top].astype(F32) + there_ref[chip, :top].astype(F32)
        ).astype(BF16)
        out_ref[chip, top:both] = here_ref[chip, top:]
        out_ref[chip, both:] = there_ref[chip, top:]


def chip_share(z, here, there):
    return pl.pallas_call(
        functools.partial(chip_share_kernel, z),
        out_shape=sds((z.chips, z.piece_slots + 2 * z.slots, LANES), BF16),
        in_specs=[VMEM, VMEM],
        out_specs=VMEM,
        compiler_params=params(16),
        cost_estimate=cost(0.5),
        name="chip_share",
    )(here, there)


def join_kernel(z, *refs):
    *parts, out_ref = refs
    top, more = z.sum_rows, parts[0].shape[0] - z.sum_rows
    sums = [ref[:top, :].astype(F32) for ref in parts]
    while len(sums) > 1:
        sums = [one + two for one, two in zip(sums[::2], sums[1::2])]
    out_ref[:top, :] = sums[0].astype(BF16)
    for p, ref in enumerate(parts):
        out_ref[top + p * more : top + (p + 1) * more, :] = ref[top:, :]


def join(z, *parts):
    rows = z.sum_rows + len(parts) * (parts[0].shape[0] - z.sum_rows)
    return pl.pallas_call(
        functools.partial(join_kernel, z),
        out_shape=sds((rows, LANES), BF16),
        in_specs=[VMEM] * len(parts),
        out_specs=VMEM,
        compiler_params=params(8),
        cost_estimate=cost(0.4),
        name="join",
    )(*parts)


def finish_kernel(z, here_ref, there_ref, lw_ref, rw_ref, gain_ref, bias_ref, out_ref):
    me = lax.axis_index(AXIS)
    top, width = z.sum_rows, z.width
    sums = here_ref[:top, :].astype(F32) + there_ref[:top, :].astype(F32)
    half = top // (z.features // LANES)
    for part in range(z.features // LANES):
        at = slice(part * LANES, (part + 1) * LANES)
        lw_ref[:, at] = sums[part * half : part * half + width]
        rw_ref[:, at] = sums[part * half + width : part * half + 2 * width]
        gain_ref[:, at] = sums[part * half + 2 * width : part * half + 2 * width + 1]
        bias_ref[:, at] = sums[part * half + 2 * width + 1 : part * half + 2 * width + 2]
    for p in range(z.size):
        ref = here_ref if p < z.size // 2 else there_ref
        first = top + (p % (z.size // 2)) * z.piece_slots
        at = pl.ds(pl.multiple_of((me ^ z.origin(p)) * z.piece, z.piece), z.piece)
        out_ref[at, :] = ref[first : first + z.piece_slots, :].astype(F32)[: z.piece]


def finish(z, here, there):
    return pl.pallas_call(
        functools.partial(finish_kernel, z),
        out_shape=(
            sds((z.width, z.features), F32),
            sds((z.width, z.features), F32),
            sds((1, z.features), F32),
            sds((1, z.features), F32),
            sds((z.width * z.width, z.pair), F32),
        ),
        in_specs=[VMEM, VMEM],
        out_specs=(VMEM,) * 5,
        compiler_params=params(8),
        cost_estimate=cost(0.9),
        name="finish",
    )(here, there)


def home_kernel(grad_ref, unit_ref, inverse_ref, gain_ref, out_ref):
    unit = unit_ref[...]
    d = grad_ref[...] * gain_ref[...]
    out_ref[...] = (
        inverse_ref[...]
        * (
            d
            - jnp.mean(d, axis=-1, keepdims=True)
            - unit * jnp.mean(d * unit, axis=-1, keepdims=True)
        )
    ).astype(BF16)


def home(z, grad, unit, inverse, gain):
    return pl.pallas_call(
        home_kernel,
        out_shape=sds(unit.shape, BF16),
        in_specs=[VMEM] * 4,
        out_specs=VMEM,
        compiler_params=params(16),
        cost_estimate=cost(1.2),
        name="home",
    )(grad, unit, inverse, gain)


def on_device(
    size,
    alignment_rows,
    norm_gain_vector,
    norm_bias_vector,
    left_weight,
    right_weight,
    output_weight,
    pair_output_gradient,
    sequence_real_mask,
    sequence_chain_index,
    residue_real_mask,
    residue_chain_index,
):
    me = lax.axis_index(AXIS)
    res, cols, pair = pair_output_gradient.shape
    features, width = left_weight.shape
    seqs = sequence_real_mask.shape[0]
    z = Sizes(size, res, cols, pair, width, features, seqs)
    same_core = [[d for d in range(size) if d % 2 == c] for c in (0, 1)]

    def swap_with(value, bit):
        return lax.ppermute(value, AXIS, [(d, d ^ bit) for d in range(size)])

    x = alignment_rows.reshape(cols, features)
    gain = norm_gain_vector.reshape(1, features)
    bias = norm_bias_vector.reshape(1, features)
    lwt, rwt = left_weight.T, right_weight.T
    left, right, unit, inverse = project(
        z, in_hbm(x), in_hbm(gain), in_hbm(bias), in_hbm(lwt), in_hbm(rwt)
    )
    left_all = lax.all_to_all(left, AXIS, 0, 0, tiled=True)

    here = right[None]
    for bit in z.masks[:-3]:
        here = stack(here, swap_with(here, bit))
    one, two = z.masks[-3:-1]
    code = (residue_chain_index + 8 * residue_real_mask).reshape(1, cols)
    code, here = lax.optimization_barrier((code, here))
    coverage, own_residues, own_sequence, w_mix = cover_all(
        z, sequence_real_mask, sequence_chain_index, code, output_weight
    )
    here = stack(here, *[swap_with(here, bit) for bit in (one, two, one ^ two)])
    mixed = mix(z, left_all, own_residues, w_mix)
    mixed, here = lax.optimization_barrier((mixed, here))
    there = swap_with(here, z.masks[-1])
    keep, give, scaled = right_sum(
        z, mixed, own_residues, coverage, pair_output_gradient
    )
    of_chip = pair_sum(keep, swap_with(give, 1))
    parts = lax.all_to_all(of_chip, AXIS, 0, 0, tiled=True, axis_index_groups=same_core)

    keep, give = left_side(z, here, there, coverage, left_all, own_residues, w_mix, scaled)
    shares = chip_share(z, keep, swap_with(give, 1))
    shares, parts = lax.optimization_barrier((shares, parts))
    got = lax.all_to_all(shares, AXIS, 0, 0, tiled=True, axis_index_groups=same_core)

    sums, grad = owner(z, parts, got, own_sequence, unit, gain, bias, lwt, rwt)
    alignment_gradient = home(z, grad, unit, inverse, gain)
    for step, bit in enumerate(z.masks[:-3]):
        there = swap_with(sums, bit)
        if step == 0:
            there, alignment_gradient = lax.optimization_barrier((there, alignment_gradient))
        sums = join(z, sums, there)
    sums = join(z, sums, *[swap_with(sums, bit) for bit in (one, two, one ^ two)])
    lw_grad, rw_grad, gain_grad, bias_grad, out_grad = finish(z, sums, swap_with(sums, z.masks[-1]))
    return (
        alignment_gradient.reshape(alignment_rows.shape),
        gain_grad.reshape(features),
        bias_grad.reshape(features),
        lw_grad.T,
        rw_grad.T,
        out_grad,
    )


def solution(mesh):
    rows = P(("grp", "dap"), None, None)
    in_specs = (rows, P(), P(), P(), P(), P(), rows, P("grp"), P("grp"), P("grp"), P("grp"))
    out_specs = (rows, P("grp"), P("grp"), P("grp", None), P("grp", None), P("grp", None))
    return jax.shard_map(
        functools.partial(on_device, mesh.shape[AXIS]),
        mesh=mesh,
        in_specs=in_specs,
        out_specs=out_specs,
        check_vma=False,
    )
```
